128 devices in a mesh: qa: 16 (over y, x), kb: 8 (over z, core).
Axes of the slice: x: 4, y: 4, z: 4, core: 2. Of those that a mesh axis runs over, the one named last changes fastest.
Arguments:
- query_rows: bfloat16 [79872, 128], P(('qa', 'kb')), may hold values from -240 to 240
- key_rows: bfloat16 [79872, 128], P(('qa', 'kb')), may hold values from -7 to 7
- value_rows: bfloat16 [79872, 128], P(('qa', 'kb')), may hold values from -6 to 6
- pair_table: int32 [16, 16], replicated, may hold values from 0 to 1, as said below
- frame_offset: int32 [16], replicated, may hold values from 0 to 47
- height_offset: int32 [16], replicated, may hold values from 0 to 15
- width_offset: int32 [16], replicated, may hold values from 0 to 15
Outputs:
- attended: bfloat16 [79872, 128], P(('qa', 'kb'))
The draws below stay inside these ranges and needn't reach their ends.
Inputs may be any that keep to these rules, and one draw needn't show every extreme that they name: pair_table[c][c] is 1, pair_table[c][d] is 0 for d > c, and entries below the diagonal are 0 or 1.
All inputs are finite; a program needn't handle non-finite values.
Results may differ from the reference program's by a relative error of at most 0.017.
Values may be sent and summed in bfloat16 or wider, within the bound.
A program may use at most 64 MiB of HBM per device.

```python
import jax
import jax.numpy as jnp
from jax import lax

HEAD = 128
HEIGHT = 32
WIDTH = 52
SPAN_LEN = 4992
SPANS = 16
TOKENS = 79872


def shared_keys(key):
    base_rows = jnp.clip(jax.random.normal(key, (TOKENS, HEAD), jnp.float32), -6.0, 6.0)
    jitter = jnp.clip(jax.random.normal(jax.random.fold_in(key, 1), (TOKENS, HEAD), jnp.float32), -6.0, 6.0)
    row_index = jnp.arange(TOKENS, dtype=jnp.int32)
    twin_rows = (row_index % 97 == 1)[:, None]
    earlier = jnp.roll(base_rows, 1, axis=0)
    return jnp.where(twin_rows, earlier + 0.1 * jitter, base_rows)


def draw_key_rows(key, part):
    shared = shared_keys(key)
    return shared.astype(jnp.bfloat16)


def draw_query_rows(key, part):
    key = jax.random.fold_in(key, 5)
    drawn_rows = 3.0 * jnp.clip(jax.random.normal(key, (TOKENS, HEAD), jnp.float32), -6.0, 6.0)
    return drawn_rows.astype(jnp.bfloat16)


def draw_pair_table(key, part):
    key = jax.random.fold_in(key, 7)
    coins = jax.random.randint(key, (SPANS, SPANS), 0, 2)
    row_index = jnp.arange(SPANS, dtype=jnp.int32)[:, None]
    column_index = jnp.arange(SPANS, dtype=jnp.int32)[None, :]
    return jnp.where(column_index == row_index, 1, jnp.where(column_index < row_index, coins, 0)).astype(jnp.int32)


def set_ends(array, key, low, top_value):
    index_at = [jax.random.randint(jax.random.fold_in(key, axis), (), 0, length) for axis, length in enumerate(array.shape)]
    longest = array.shape.index(max(array.shape))
    next_to = index_at[:longest] + [(index_at[longest] + 1) % array.shape[longest]] + index_at[longest + 1:]
    return array.at[tuple(index_at)].set(low).at[tuple(next_to)].set(top_value)


def block_levels(stream_key, shape, shards, low, largest):
    def one(dim, parts):
        steps = jax.random.uniform(jax.random.fold_in(jax.random.fold_in(stream_key, 6), dim), (parts,), jnp.float32, low / len(shards), largest / len(shards))
        return jnp.repeat(jnp.exp(steps), shape[dim] // parts).reshape((-1,) + (1,) * (len(shape) - dim - 1))

    factor_of = one(*shards[0])
    for cut in shards[1:]:
        factor_of = factor_of * one(*cut)
    return factor_of


def scatter_about(rng, extent, scale, most, cuts=(), kind=jnp.bfloat16):
    gain = block_levels(rng, extent, cuts, -0.22, 0.18) if cuts else 1.0
    values = jax.random.normal(rng, extent, jnp.float32) * scale * gain
    return jnp.minimum(jnp.maximum(values, -most), most).astype(kind)


def setup_inputs(seed: int = 0) -> dict:
    key_list = jax.random.split(jax.random.key(seed), 8)
    return {
        "query_rows": draw_query_rows(jax.random.fold_in(key_list[7], 71), 0),
        "key_rows": draw_key_rows(jax.random.fold_in(key_list[7], 71), 0),
        "value_rows": scatter_about(key_list[2], (TOKENS, HEAD), 1.0, 6.0, ((0, 128),)),
        "pair_table": draw_pair_table(jax.random.fold_in(key_list[7], 71), 0),
        "frame_offset": set_ends(jax.random.randint(key_list[4], (SPANS,), 0, 48), jax.random.fold_in(key_list[4], 1), 0, 47).astype(jnp.int32),
        "height_offset": set_ends(jax.random.randint(key_list[5], (SPANS,), 0, 16), jax.random.fold_in(key_list[5], 1), 0, 15).astype(jnp.int32),
        "width_offset": set_ends(jax.random.randint(key_list[6], (SPANS,), 0, 16), jax.random.fold_in(key_list[6], 1), 0, 15).astype(jnp.int32),
    }


def angle_table(frame_pos, height_pos, width_pos, head_size):
    pair_count = head_size // 2
    side_count = pair_count // 3
    lead_count = pair_count - 2 * side_count

    def frequency(number):
        return 1.0 / (10000.0 ** (jnp.arange(number, dtype=jnp.float32) / number))

    return jnp.concatenate([
        frame_pos.astype(jnp.float32)[:, None] * frequency(lead_count)[None, :],
        height_pos.astype(jnp.float32)[:, None] * frequency(side_count)[None, :],
        width_pos.astype(jnp.float32)[:, None] * frequency(side_count)[None, :]], axis=1)


def rotate(rows_in, angles):
    half_cols = rows_in.shape[1] // 2
    leading = rows_in[:, :half_cols].astype(jnp.float32)
    trailing = rows_in[:, half_cols:].astype(jnp.float32)
    cosine = jnp.cos(angles)
    sine = jnp.sin(angles)
    return jnp.concatenate([leading * cosine - trailing * sine, leading * sine + trailing * cosine], axis=1).astype(jnp.bfloat16)


def reference(query_rows, key_rows, value_rows, pair_table, frame_offset, height_offset, width_offset):
    token = jnp.arange(TOKENS, dtype=jnp.int32)
    span_ids = token // SPAN_LEN
    within = token % SPAN_LEN
    frame_pos = within // (HEIGHT * WIDTH) + frame_offset[span_ids]
    height_pos = (within // WIDTH) % HEIGHT + height_offset[span_ids]
    width_pos = within % WIDTH + width_offset[span_ids]
    angles = angle_table(frame_pos, height_pos, width_pos, HEAD)
    query_turned = rotate(query_rows, angles).reshape(SPANS, SPAN_LEN, HEAD)
    key_turned = rotate(key_rows, angles).reshape(SPANS, SPAN_LEN, HEAD)
    value_spans = value_rows.reshape(SPANS, SPAN_LEN, HEAD)
    score_scale = float(HEAD) ** -0.5

    def scores_of(query_span, key_span):
        return lax.dot_general(query_span, key_span, (((1,), (1,)), ((), ())),
                               preferred_element_type=jnp.float32) * score_scale

    def per_span(span_index):
        query_span = query_turned[span_index]

        def max_step(maxima, key_index):
            allowed = pair_table[span_index, key_index] > 0
            maxima = lax.cond(allowed,
                              lambda present: jnp.maximum(present, jnp.max(scores_of(query_span, key_turned[key_index]), axis=1)),
                              lambda present: present, maxima)
            return maxima, None

        start_max = jnp.full((SPAN_LEN,), -1e30, jnp.float32)
        maxima, unused = lax.scan(max_step, start_max, jnp.arange(SPANS, dtype=jnp.int32))

        def sum_step(running, key_index):
            allowed = pair_table[span_index, key_index] > 0

            def add_pair(present):
                totals, numerators = present
                weights = jnp.exp(scores_of(query_span, key_turned[key_index]) - maxima[:, None])
                totals = totals + jnp.sum(weights, axis=1)
                numerators = numerators + jnp.dot(weights.astype(jnp.bfloat16), value_spans[key_index],
                                                  preferred_element_type=jnp.float32)
                return totals, numerators

            return lax.cond(allowed, add_pair, lambda present: present, running), None

        start_sums = (jnp.zeros((SPAN_LEN,), jnp.float32), jnp.zeros((SPAN_LEN, HEAD), jnp.float32))
        sums, unused = lax.scan(sum_step, start_sums, jnp.arange(SPANS, dtype=jnp.int32))
        return (sums[1] / sums[0][:, None]).astype(jnp.bfloat16)

    attended = lax.map(per_span, jnp.arange(SPANS, dtype=jnp.int32))
    return attended.reshape(TOKENS, HEAD)
```

```python
import functools
import jax
import jax.numpy as jnp
import numpy as np
from jax import lax
from jax.experimental import pallas as pl
from jax.experimental.pallas import tpu as pltpu
from jax.sharding import PartitionSpec as P

HEIGHT = 32
WIDTH = 52
SPANS = 16
TILE = 624
HEAD = 128
PIECE = 80
STARTS = tuple(16 * (i * 34 // 7) for i in range(8))
MESH = pl.DeviceIdType.MESH
BF16 = jnp.bfloat16
F32 = jnp.float32
ROWS = 4 * PIECE
UNROLL = 4
SCALE = float(HEAD ** -0.5)
SCALE2 = float(HEAD ** -0.5 * np.log2(np.e))
LIMIT = 72.0


def coords():
    qa = lax.axis_index("qa")
    kb = lax.axis_index("kb")
    return qa, kb, kb // 2, kb % 2


def turn_table(freq_ref, fo_ref, ho_ref, wo_ref, qa, kb):
    row = lax.broadcasted_iota(jnp.int32, (TILE, HEAD), 0)
    lane = lax.broadcasted_iota(jnp.int32, (TILE, HEAD), 1) % 64
    within = (row + kb * TILE).astype(F32)
    frame = jnp.floor((within + 0.5) * (1.0 / (HEIGHT * WIDTH)))
    line = jnp.floor((within + 0.5) * (1.0 / WIDTH))
    column = within - line * WIDTH + wo_ref[qa].astype(F32)
    line = line - frame * HEIGHT + ho_ref[qa].astype(F32)
    frame = frame + fo_ref[qa].astype(F32)
    angles = jnp.where(lane < 22, frame, jnp.where(lane < 43, line, column)) * freq_ref[...]
    turns = jnp.floor(angles * np.float32(2 / np.pi) + 0.5)
    rest = angles - turns * np.float32(1.5703125)
    rest = rest - turns * np.float32(4.837512969970703125e-4)
    rest = rest - turns * np.float32(7.54978995489188216e-8)
    sq = rest * rest
    sine = rest + rest * sq * (np.float32(-1 / 6) + sq * (np.float32(8.3333333e-3) + sq * (np.float32(-1.98412698e-4) + sq * np.float32(2.7525562e-6))))
    cosine = 1.0 + sq * (np.float32(-0.5) + sq * (np.float32(4.16666667e-2) + sq * (np.float32(-1.38888889e-3) + sq * (np.float32(2.48015873e-5) + sq * np.float32(-2.7557319e-7)))))
    half = jnp.floor(turns * 0.5)
    odd = (turns - 2.0 * half) > 0.5
    flip = (half - 2.0 * jnp.floor(half * 0.5)) > 0.5
    sign = jnp.where(flip, -1.0, 1.0)
    cos_out = jnp.where(odd, -sine, cosine) * sign
    sin_out = jnp.where(odd, cosine, sine) * sign
    full_lane = lax.broadcasted_iota(jnp.int32, (TILE, HEAD), 1)
    return cos_out, jnp.where(full_lane < 64, -sin_out, sin_out)


def turn(rows, cos_out, sin_out):
    x = rows.astype(F32)
    return (x * cos_out + pltpu.roll(x, 64, 1) * sin_out).astype(BF16)


def longest(rows):
    x = rows.astype(F32)
    return jnp.max(jnp.sum(x * x, axis=1, keepdims=True), axis=0, keepdims=True)


def move_kernel(q_ref, k_ref, v_ref, freq_ref, fo_ref, ho_ref, wo_ref, qg, kv, bound,
                qs, q_send, q_recv, z_send, z_recv, s_send, s_recv, kv_send, kv_recv, local_sem):
    qa, kb, z, core = coords()
    step_a = 1 + 3 * core
    step_b = 4 - 3 * core
    a = (qa // step_a) % 4
    b = (qa // step_b) % 4
    primary = (qa // 8) == core

    def at(aa, bb):
        return (aa % 4) * step_a + (bb % 4) * step_b

    barrier = pltpu.get_barrier_semaphore()
    for d in range(1, SPANS):
        pl.semaphore_signal(barrier, inc=1, device_id=((qa + d) % SPANS, kb), device_id_type=MESH)
    for other in ((kb + 2) % 8, (kb + 6) % 8, z * 2 + 1 - core):
        pl.semaphore_signal(barrier, inc=1, device_id=(qa, other), device_id_type=MESH)
    cos_out, sin_out = turn_table(freq_ref, fo_ref, ho_ref, wo_ref, qa, kb)
    qs[...] = turn(q_ref[...], cos_out, sin_out)
    kv[qa, 0] = turn(k_ref[...], cos_out, sin_out)
    kv[qa, 1] = v_ref[...]
    pl.semaphore_wait(barrier, 18)

    def remote(src, dst, send, recv, device):
        return pltpu.make_async_remote_copy(src_ref=src, dst_ref=dst, send_sem=send, recv_sem=recv, device_id=device, device_id_type=MESH)

    q_copies = []
    for i in range(8):
        r = 8 * core + i
        q_copies.append((r, remote(qs.at[pl.ds(STARTS[i], PIECE)], qg.at[z, qa], q_send.at[i], q_recv.at[qa], (r, kb))))
    for r, copy in q_copies:
        @pl.when(r != qa)
        def _():
            copy.start()
    for i in range(8):
        @pl.when(8 * core + i == qa)
        def _():
            own = pltpu.make_async_copy(qs.at[pl.ds(STARTS[i], PIECE)], qg.at[z, qa], local_sem)
            own.start()
            own.wait()

    sends = []
    count = [0]

    def kv_copy(src, part, recv_index, device):
        n = count[0]
        count[0] += 1
        ref = kv.at[src] if part is None else kv.at[src, part]
        copy = remote(ref, ref, kv_send.at[n], kv_recv.at[recv_index], device)
        copy.start()
        sends.append(copy)

    def kv_wait(src, part, recv_index):
        ref = kv.at[src] if part is None else kv.at[src, part]
        remote(ref, ref, kv_send.at[0], kv_recv.at[recv_index], (qa, kb)).wait_recv()

    up_a, down_a = (at(a + 1, b), kb), (at(a - 1, b), kb)
    up_b, down_b = (at(a, b + 1), kb), (at(a, b - 1), kb)
    kv_copy(qa, None, 0, up_a)
    kv_copy(qa, None, 1, down_a)

    def second(item, aa):
        kv_copy(at(aa, b), None, 4 + 4 * item, up_b)
        kv_copy(at(aa, b), None, 5 + 4 * item, down_b)

    second(0, a)

    up_z, down_z, twin = (qa, (kb + 2) % 8), (qa, (kb + 6) % 8), (qa, z * 2 + 1 - core)
    low, high = pl.ds(0, 8), pl.ds(8, 8)
    zm, zp, zo = (z + 3) % 4, (z + 1) % 4, (z + 2) % 4

    def zc(quarter, rows, sem, recv, device):
        ref = qg.at[quarter] if rows is None else qg.at[quarter, rows]
        return remote(ref, ref, sem[0].at[sem[1]], recv[0].at[recv[1]], device)

    @pl.when(primary)
    def _():
        for c in range(SPANS):
            @pl.when(c != qa)
            def _():
                remote(qs.at[pl.ds(0, PIECE)], qg.at[z, c], q_send.at[0], q_recv.at[c], (qa, kb)).wait_recv()
        zc(z, None, (z_send, 0), (z_recv, 0), up_z).start()
        zc(z, None, (z_send, 1), (z_recv, 1), down_z).start()
        zc(z, None, (s_send, 0), (s_recv, 0), twin).start()

    reach = [longest(kv[qa, 0])]

    def look(block):
        reach[0] = jnp.maximum(reach[0], longest(kv[block, 0]))

    kv_wait(at(a - 1, b), None, 0)
    kv_copy(at(a - 1, b), 0, 2, up_a)
    second(1, a - 1)
    kv_wait(at(a + 1, b), None, 1)
    kv_copy(at(a + 1, b), 1, 3, down_a)
    second(2, a + 1)
    look(at(a - 1, b))
    look(at(a + 1, b))

    @pl.when(primary)
    def _():
        zc(zm, None, (z_send, 0), (z_recv, 0), up_z).wait_recv()
        zc(zm, low, (z_send, 2), (z_recv, 2), up_z).start()
        zc(zm, None, (s_send, 1), (s_recv, 1), twin).start()
        zc(zp, None, (z_send, 1), (z_recv, 1), down_z).wait_recv()
        zc(zp, high, (z_send, 3), (z_recv, 3), down_z).start()
        zc(zp, None, (s_send, 2), (s_recv, 2), twin).start()

    kv_wait(at(a + 2, b), 0, 2)
    kv_wait(at(a + 2, b), 1, 3)
    second(3, a + 2)
    look(at(a + 2, b))

    @pl.when(primary)
    def _():
        zc(zo, low, (z_send, 2), (z_recv, 2), up_z).wait_recv()
        zc(zo, high, (z_send, 3), (z_recv, 3), down_z).wait_recv()
        zc(zo, None, (s_send, 3), (s_recv, 3), twin).start()

    items = ((0, a), (1, a - 1), (2, a + 1), (3, a + 2))
    for item, aa in items:
        kv_wait(at(aa, b - 1), None, 4 + 4 * item)
        kv_copy(at(aa, b - 1), 0, 6 + 4 * item, up_b)
        kv_wait(at(aa, b + 1), None, 5 + 4 * item)
        kv_copy(at(aa, b + 1), 1, 7 + 4 * item, down_b)
        look(at(aa, b - 1))
        look(at(aa, b + 1))
    for item, aa in items:
        kv_wait(at(aa, b + 2), 0, 6 + 4 * item)
        kv_wait(at(aa, b + 2), 1, 7 + 4 * item)
        look(at(aa, b + 2))

    @pl.when(jnp.logical_not(primary))
    def _():
        for n, quarter in enumerate((z, zm, zp, zo)):
            zc(quarter, None, (s_send, n), (s_recv, n), twin).wait_recv()

    def stretch(c, best):
        for quarter in range(4):
            best = jnp.maximum(best, longest(qg[quarter, c]))
        return best

    far = lax.fori_loop(0, SPANS, stretch, jnp.zeros((1, 1), F32))
    bound[...] = jnp.broadcast_to(jnp.sqrt(far * reach[0]) * SCALE, bound.shape)

    @pl.when(primary)
    def _():
        zc(z, None, (z_send, 0), (z_recv, 0), up_z).wait_send()
        zc(z, None, (z_send, 1), (z_recv, 1), down_z).wait_send()
        zc(zm, low, (z_send, 2), (z_recv, 2), up_z).wait_send()
        zc(zp, high, (z_send, 3), (z_recv, 3), down_z).wait_send()
        for n, quarter in enumerate((z, zm, zp, zo)):
            zc(quarter, None, (s_send, n), (s_recv, n), twin).wait_send()
    for r, copy in q_copies:
        @pl.when(r != qa)
        def _():
            copy.wait_send()
    for copy in sends:
        copy.wait_send()


def frequencies():
    lead = 1.0 / 10000.0 ** (np.arange(22, dtype=np.float32) / np.float32(22))
    side = 1.0 / 10000.0 ** (np.arange(21, dtype=np.float32) / np.float32(21))
    one = np.concatenate([lead, side, side]).astype(np.float32)
    return jnp.asarray(np.concatenate([one, one])[None])


def move(q, k, v, fo, ho, wo):
    dma = pltpu.SemaphoreType.DMA
    vmem = pl.BlockSpec(memory_space=pltpu.VMEM)
    smem = pl.BlockSpec(memory_space=pltpu.SMEM)
    return pl.pallas_call(
        move_kernel,
        out_shape=[jax.ShapeDtypeStruct((4, SPANS, PIECE, HEAD), BF16), jax.ShapeDtypeStruct((SPANS, 2, TILE, HEAD), BF16),
                   jax.ShapeDtypeStruct((8, HEAD), F32)],
        in_specs=[vmem] * 4 + [smem] * 3,
        out_specs=[vmem, vmem, vmem],
        scratch_shapes=[pltpu.VMEM((TILE, HEAD), BF16), dma((8,)), dma((16,)), dma((4,)), dma((4,)), dma((4,)), dma((4,)), dma((20,)), dma((20,)), dma(())],
        compiler_params=pltpu.CompilerParams(collective_id=0, has_side_effects=True, vmem_limit_bytes=40 << 20),
    )(q, k, v, frequencies(), fo, ho, wo)


def column_to_row(column):
    eye = lax.broadcasted_iota(jnp.int32, column.shape, 0) == lax.broadcasted_iota(jnp.int32, column.shape, 1)
    return jnp.sum(jnp.where(eye, column, 0.0), axis=0, keepdims=True)


def encode(row):
    first = row.astype(BF16).astype(F32)
    second = (row - first).astype(BF16).astype(F32)
    third = (row - first - second).astype(BF16).astype(F32)
    place = lax.broadcasted_iota(jnp.int32, (16, HEAD), 0)
    tile = jnp.where(place == 0, first, jnp.where(place == 1, second, jnp.where(place == 2, third, 0.0)))
    return tile.astype(BF16)


def attend_kernel(table, bound, qg, kv, out, acc, top, cells):
    total = jnp.int32(0)
    for c in range(SPANS):
        for d in range(c + 1):
            cells[total] = c * SPANS + d
            total = total + table[c, d]
    for n in range(UNROLL - 1):
        cells[total + n] = SPANS * SPANS
    acc[...] = jnp.zeros_like(acc)
    ones = jnp.ones((TILE, HEAD), BF16)
    safe = jnp.max(bound[...]) <= LIMIT

    def operands(n):
        code = cells[n]
        c = code // SPANS
        d = code % SPANS
        cc = jnp.minimum(c, SPANS - 1)
        q = jnp.concatenate([qg[i, cc] for i in range(4)], axis=0)
        s = lax.dot_general(q, kv[d, 0], (((1,), (1,)), ((), ())), preferred_element_type=F32)
        return c, s, jnp.concatenate([kv[d, 1], ones], axis=1)

    @pl.when(safe)
    def _():
        @pl.loop(0, (total + UNROLL - 1) // UNROLL)
        def _(step):
            for u in range(UNROLL):
                c, s, v = operands(step * UNROLL + u)
                p = jnp.exp2(s * SCALE2).astype(BF16)
                acc[c] += jnp.dot(p, v, preferred_element_type=F32)

    @pl.when(jnp.logical_not(safe))
    def _():
        top[...] = jnp.full_like(top, -1e30)

        @pl.loop(0, total)
        def _(n):
            c, s, v = operands(n)
            s = s * SCALE
            old = top[c]
            new = jnp.maximum(old, jnp.max(s, axis=1, keepdims=True))
            p = jnp.exp(s - new[:, 0:1]).astype(BF16)
            shrink = jnp.exp(old - new)
            acc[c] = acc[c] * jnp.concatenate([shrink, shrink], axis=1) + jnp.dot(p, v, preferred_element_type=F32)
            top[c] = new

    @pl.loop(0, SPANS)
    def _(c):
        for i in range(4):
            rows = pl.ds(i * PIECE, PIECE)
            sums = acc[c, rows, HEAD:]
            out[i, c, 0:PIECE] = (acc[c, rows, :HEAD] / sums).astype(BF16)
            level = jnp.log(sums) + jnp.where(safe, 0.0, top[c, rows])
            out[i, c, PIECE:] = encode(column_to_row(level))


def attend(table, bound, qg, kv):
    vmem = pl.BlockSpec(memory_space=pltpu.VMEM)
    smem = pl.BlockSpec(memory_space=pltpu.SMEM)
    return pl.pallas_call(
        attend_kernel,
        out_shape=jax.ShapeDtypeStruct((4, SPANS, PIECE + 16, HEAD), BF16),
        in_specs=[smem, vmem, vmem, vmem],
        out_specs=vmem,
        scratch_shapes=[pltpu.VMEM((SPANS + 1, ROWS, 2 * HEAD), F32), pltpu.VMEM((SPANS + 1, ROWS, HEAD), F32), pltpu.SMEM((160,), jnp.int32)],
        compiler_params=pltpu.CompilerParams(vmem_limit_bytes=40 << 20),
    )(table, bound, qg, kv)


def read_rows(block):
    parts = block.astype(F32)
    return parts[0:1] + parts[1:2] + parts[2:3]


def row_to_column(row):
    eye = lax.broadcasted_iota(jnp.int32, (PIECE, HEAD), 0) == lax.broadcasted_iota(jnp.int32, (PIECE, HEAD), 1)
    return jnp.sum(jnp.where(eye, jnp.broadcast_to(row, (PIECE, HEAD)), 0.0), axis=1, keepdims=True)


def merge_kernel(part, out, from_twin, merged, arrived, t_send, t_recv, m_send, m_recv, local_sem):
    qa, kb, z, core = coords()
    home = qa // 8
    twin = (qa, z * 2 + 1 - core)
    mine = pl.ds(8 * core, 8)
    other = pl.ds(8 - 8 * core, 8)
    me_too = jnp.where(home == core, 1, 0)
    slot = qa % 8

    barrier = pltpu.get_barrier_semaphore()
    pl.semaphore_signal(barrier, inc=1, device_id=twin, device_id_type=MESH)
    for i in range(8):
        for zz in range(4):
            @pl.when(jnp.logical_or(8 * core + i != qa, zz * 2 + home != kb))
            def _():
                pl.semaphore_signal(barrier, inc=1, device_id=(8 * core + i, zz * 2 + home), device_id_type=MESH)
    pl.semaphore_wait(barrier, 33 - me_too)

    def remote(src, dst, send, recv, device):
        return pltpu.make_async_remote_copy(src_ref=src, dst_ref=dst, send_sem=send, recv_sem=recv, device_id=device, device_id_type=MESH)

    def swap(n):
        zz = (z + n) % 4
        return remote(part.at[zz, other], from_twin.at[zz], t_send.at[n], t_recv.at[n], twin)

    def give(n, i):
        zz = (z + n) % 4
        return remote(merged.at[zz, i], arrived.at[slot, z], m_send.at[n, i], m_recv.at[slot, z], (8 * core + i, zz * 2 + home))

    order = (2, 1, 3, 0)
    for n in order:
        swap(n).start()
    for n in order:
        zz = (z + n) % 4
        swap(n).wait_recv()
        for i in range(8):
            level_0 = read_rows(part[zz, 8 * core + i, PIECE:])
            level_1 = read_rows(from_twin[zz, i, PIECE:])
            peak = jnp.maximum(level_0, level_1)
            level = peak + jnp.log(jnp.exp(level_0 - peak) + jnp.exp(level_1 - peak))
            share = row_to_column(jnp.exp(level_0 - level))
            x0 = part[zz, 8 * core + i, 0:PIECE].astype(F32)
            x1 = from_twin[zz, i, 0:PIECE].astype(F32)
            merged[zz, i, 0:PIECE] = (x1 + share * (x0 - x1)).astype(BF16)
            merged[zz, i, PIECE:] = encode(level)
            if n == 0:
                @pl.when(8 * core + i != qa)
                def _():
                    give(n, i).start()

                @pl.when(8 * core + i == qa)
                def _():
                    pass
            else:
                give(n, i).start()

    @pl.when(home == core)
    def _():
        keep = pltpu.make_async_copy(merged.at[z, slot], arrived.at[slot, z], local_sem)
        keep.start()
        keep.wait()
    for i in range(8):
        for zz in range(4):
            @pl.when(jnp.logical_or(8 * core + i != qa, zz * 2 + home != kb))
            def _():
                remote(merged.at[0, 0], arrived.at[i, zz], m_send.at[0, 0], m_recv.at[i, zz], (8 * core + i, zz * 2 + home)).wait_recv()
        levels = [read_rows(arrived[i, zz, PIECE:]) for zz in range(4)]
        peak = jnp.maximum(jnp.maximum(levels[0], levels[1]), jnp.maximum(levels[2], levels[3]))
        weights = [jnp.exp(level - peak) for level in levels]
        total = weights[0] + weights[1] + weights[2] + weights[3]
        value = None
        for zz in range(4):
            term = row_to_column(weights[zz] / total) * arrived[i, zz, 0:PIECE].astype(F32)
            value = term if value is None else value + term
        out[STARTS[i]:STARTS[i] + PIECE] = value.astype(BF16)

    for n in order:
        swap(n).wait_send()
        for i in range(8):
            if n == 0:
                @pl.when(8 * core + i != qa)
                def _():
                    give(n, i).wait_send()
            else:
                give(n, i).wait_send()


def merge(part):
    dma = pltpu.SemaphoreType.DMA
    vmem = pl.BlockSpec(memory_space=pltpu.VMEM)
    block = (PIECE + 16, HEAD)
    return pl.pallas_call(
        merge_kernel,
        out_shape=jax.ShapeDtypeStruct((TILE, HEAD), BF16),
        in_specs=[vmem],
        out_specs=vmem,
        scratch_shapes=[pltpu.VMEM((4, 8) + block, BF16), pltpu.VMEM((4, 8) + block, BF16), pltpu.VMEM((8, 4) + block, BF16),
                        dma((4,)), dma((4,)), dma((4, 8)), dma((8, 4)), dma(())],
        compiler_params=pltpu.CompilerParams(collective_id=1, has_side_effects=True, vmem_limit_bytes=40 << 20),
    )(part)


def local(q, k, v, table, fo, ho, wo):
    qg, kv, bound = move(q, k, v, fo, ho, wo)
    return merge(attend(table, bound, qg, kv))


def solution(mesh):
    S = P(("qa", "kb"), None)
    return jax.shard_map(local, mesh=mesh, in_specs=(S, S, S, P(), P(), P(), P()), out_specs=S, check_vma=False)
```

```python
import jax
import jax.numpy as jnp
import numpy as np
from jax import lax
from jax.experimental import pallas as pl
from jax.experimental.pallas import tpu as pltpu
from jax.sharding import PartitionSpec as P

HEIGHT = 32
WIDTH = 52
SPANS = 16
TILE = 624
HEAD = 128
PIECE = 80
STARTS = tuple(16 * (i * 34 // 7) for i in range(8))
MESH = pl.DeviceIdType.MESH
BF16 = jnp.bfloat16
F32 = jnp.float32
ROWS = 2 * PIECE
KEYS = 2 * TILE
UNROLL = 4
SCALE = float(HEAD ** -0.5)
SCALE2 = float(HEAD ** -0.5 * np.log2(np.e))
LIMIT = 72.0


def coords():
    qa = lax.axis_index("qa")
    kb = lax.axis_index("kb")
    return qa, kb, kb // 2, kb % 2


def turn_table(freq_ref, fo_ref, ho_ref, wo_ref, qa, kb):
    row = lax.broadcasted_iota(jnp.int32, (TILE, HEAD), 0)
    lane = lax.broadcasted_iota(jnp.int32, (TILE, HEAD), 1) % 64
    within = (row + kb * TILE).astype(F32)
    frame = jnp.floor((within + 0.5) * (1.0 / (HEIGHT * WIDTH)))
    line = jnp.floor((within + 0.5) * (1.0 / WIDTH))
    column = within - line * WIDTH + wo_ref[qa].astype(F32)
    line = line - frame * HEIGHT + ho_ref[qa].astype(F32)
    frame = frame + fo_ref[qa].astype(F32)
    angles = jnp.where(lane < 22, frame, jnp.where(lane < 43, line, column)) * freq_ref[...]
    turns = jnp.floor(angles * np.float32(2 / np.pi) + 0.5)
    rest = angles - turns * np.float32(1.5703125)
    rest = rest - turns * np.float32(4.837512969970703125e-4)
    rest = rest - turns * np.float32(7.54978995489188216e-8)
    sq = rest * rest
    sine = rest + rest * sq * (np.float32(-1 / 6) + sq * (np.float32(8.3333333e-3) + sq * (np.float32(-1.98412698e-4) + sq * np.float32(2.7525562e-6))))
    cosine = 1.0 + sq * (np.float32(-0.5) + sq * (np.float32(4.16666667e-2) + sq * (np.float32(-1.38888889e-3) + sq * (np.float32(2.48015873e-5) + sq * np.float32(-2.7557319e-7)))))
    half = jnp.floor(turns * 0.5)
    odd = (turns - 2.0 * half) > 0.5
    flip = (half - 2.0 * jnp.floor(half * 0.5)) > 0.5
    sign = jnp.where(flip, -1.0, 1.0)
    cos_out = jnp.where(odd, -sine, cosine) * sign
    sin_out = jnp.where(odd, cosine, sine) * sign
    full_lane = lax.broadcasted_iota(jnp.int32, (TILE, HEAD), 1)
    return cos_out, jnp.where(full_lane < 64, -sin_out, sin_out)


def turn(rows, cos_out, sin_out):
    x = rows.astype(F32)
    return (x * cos_out + pltpu.roll(x, 64, 1) * sin_out).astype(BF16)


def longest(rows):
    x = rows.astype(F32)
    return jnp.max(jnp.sum(x * x, axis=1, keepdims=True), axis=0, keepdims=True)


def remote(src, dst, send, recv, device):
    return pltpu.make_async_remote_copy(src_ref=src, dst_ref=dst, send_sem=send, recv_sem=recv, device_id=device, device_id_type=MESH)


def move_kernel(q_in, k_in, v_in, freq_in, fo_in, ho_in, wo_in, qg, kv, bound,
                qs, ks, freq, fo, ho, wo, in_sem, q_send, q_recv, z_send, z_recv, kv_send, kv_recv, t_send, t_recv, local_sem):
    qa, kb, z, core = coords()
    step_a = 1 + 3 * core
    step_b = 4 - 3 * core
    a = (qa // step_a) % 4
    b = (qa // step_b) % 4
    entry = z // 2 == core
    twin = (qa, z * 2 + 1 - core)
    mine = pl.ds(core * TILE, TILE)

    def at(aa, bb):
        return (aa % 4) * step_a + (bb % 4) * step_b

    barrier = pltpu.get_barrier_semaphore()
    loads = [pltpu.make_async_copy(src, dst, in_sem.at[n]) for n, (src, dst) in enumerate((
        (freq_in, freq), (fo_in, fo), (ho_in, ho), (wo_in, wo), (q_in, qs), (k_in, ks), (v_in, kv.at[qa, 1, mine])))]
    for load in loads:
        load.start()
    for d in range(1, SPANS):
        other = (qa + d) % SPANS
        pl.semaphore_signal(barrier, inc=1, device_id=(other, kb), device_id_type=MESH)
        pl.semaphore_signal(barrier, inc=1, device_id=(other, z * 2 + 1 - core), device_id_type=MESH)
    pl.semaphore_signal(barrier, inc=1, device_id=twin, device_id_type=MESH)
    for d in range(1, 4):
        pl.semaphore_signal(barrier, inc=1, device_id=(qa, (kb + 2 * d) % 8), device_id_type=MESH)
    for load in loads:
        load.wait()
    cos_out, sin_out = turn_table(freq, fo, ho, wo, qa, kb)
    qs[...] = turn(qs[...], cos_out, sin_out)
    kv[qa, 0, mine] = turn(ks[...], cos_out, sin_out)
    pl.semaphore_wait(barrier, 34)

    def q_copy(i):
        return remote(qs.at[pl.ds(STARTS[i], PIECE)], qg.at[z % 2, qa], q_send.at[i], q_recv.at[qa], (8 * core + i, z * 2 + z // 2))

    def is_me(i):
        return jnp.logical_and(8 * core + i == qa, entry)

    for i in range(8):
        @pl.when(jnp.logical_not(is_me(i)))
        def _():
            q_copy(i).start()

        @pl.when(is_me(i))
        def _():
            own = pltpu.make_async_copy(qs.at[pl.ds(STARTS[i], PIECE)], qg.at[z % 2, qa], local_sem)
            own.start()
            own.wait()

    sends = []
    count = [0]

    def part_ref(span, part):
        return kv.at[span, part, mine]

    def kv_copy(span, part, device):
        copy = remote(part_ref(span, part), part_ref(span, part), kv_send.at[count[0]], kv_recv.at[span, part], device)
        count[0] += 1
        copy.start()
        sends.append(copy)

    def kv_wait(span, part):
        remote(part_ref(span, part), part_ref(span, part), kv_send.at[0], kv_recv.at[span, part], twin).wait_recv()

    def twin_copy(span, part):
        return remote(part_ref(span, part), part_ref(span, part), t_send.at[span, part], t_recv.at[span, part], twin)

    up_a, down_a = (at(a + 1, b), kb), (at(a - 1, b), kb)
    up_b, down_b = (at(a, b + 1), kb), (at(a, b - 1), kb)
    for part in (1, 0):
        for device in (up_a, down_a, up_b, down_b):
            kv_copy(qa, part, device)
        twin_copy(qa, part).start()

    def z_copy(d):
        return remote(qg.at[z % 2], qg.at[z % 2], z_send.at[d - 1], z_recv.at[z % 2], (qa, (kb + 2 * d) % 8))

    @pl.when(entry)
    def _():
        for c in range(SPANS):
            @pl.when(jnp.logical_or(c != qa, qa // 8 != core))
            def _():
                remote(qs.at[pl.ds(0, PIECE)], qg.at[z % 2, c], q_send.at[0], q_recv.at[c], twin).wait_recv()
        for d in (2, 1, 3):
            z_copy(d).start()

    def arrive(span, part, devices):
        kv_wait(span, part)
        for device in devices:
            kv_copy(span, part, device)
        twin_copy(span, part).start()

    arrive(at(a - 1, b), 1, (up_a, up_b, down_b))
    arrive(at(a + 1, b), 1, (up_b, down_b))
    arrive(at(a, b - 1), 1, (up_b,))
    arrive(at(a, b + 1), 1, ())
    arrive(at(a - 1, b), 0, (up_b, down_b))
    arrive(at(a + 1, b), 0, (down_a, up_b, down_b))
    arrive(at(a, b - 1), 0, ())
    arrive(at(a, b + 1), 0, (down_b,))
    arrive(at(a + 2, b), 1, (up_b, down_b))
    arrive(at(a + 2, b), 0, (up_b, down_b))
    reach = [longest(kv[qa, 0, mine])]

    def look(span):
        reach[0] = jnp.maximum(reach[0], longest(kv[span, 0, mine]))

    for step in (3, 1, 2):
        look(at(a + step, b))
    for step in (3, 1, 2):
        arrive(at(a + step, b - 1), 1, (up_b,))
        arrive(at(a + step, b + 1), 1, ())
        arrive(at(a + step, b - 1), 0, ())
        arrive(at(a + step, b + 1), 0, (down_b,))
        look(at(a + step, b - 1))
        look(at(a + step, b + 1))
    for step in (0, 3, 1, 2):
        arrive(at(a + step, b + 2), 1, ())
        arrive(at(a + step, b + 2), 0, ())
        look(at(a + step, b + 2))

    for span in range(SPANS):
        for part in (1, 0):
            ref = kv.at[span, part, pl.ds((1 - core) * TILE, TILE)]
            remote(ref, ref, t_send.at[0, 0], t_recv.at[span, part], twin).wait_recv()

    for half in range(2):
        @pl.when(jnp.logical_or(jnp.logical_not(entry), half != z % 2))
        def _():
            remote(qg.at[half], qg.at[half], z_send.at[0], z_recv.at[half], twin).wait_recv()

    def other_look(span, best):
        return jnp.maximum(best, longest(kv[span, 0, pl.ds(pl.multiple_of((1 - core) * TILE, 16), TILE)]))

    def stretch(c, best):
        return jnp.maximum(best, jnp.maximum(longest(qg[0, c]), longest(qg[1, c])))

    reach[0] = lax.fori_loop(0, SPANS, other_look, reach[0])
    far = lax.fori_loop(0, SPANS, stretch, jnp.zeros((1, 1), F32))
    bound[...] = jnp.broadcast_to(jnp.sqrt(far * reach[0]) * SCALE, bound.shape)

    @pl.when(entry)
    def _():
        for d in (1, 2, 3):
            z_copy(d).wait_send()
    for i in range(8):
        @pl.when(jnp.logical_not(is_me(i)))
        def _():
            q_copy(i).wait_send()
    for copy in sends:
        copy.wait_send()
    for span in range(SPANS):
        for part in (1, 0):
            twin_copy(span, part).wait_send()


def frequencies():
    lead = 1.0 / 10000.0 ** (np.arange(22, dtype=np.float32) / np.float32(22))
    side = 1.0 / 10000.0 ** (np.arange(21, dtype=np.float32) / np.float32(21))
    one = np.concatenate([lead, side, side]).astype(np.float32)
    return jnp.asarray(np.concatenate([one, one])[None])


def move(q, k, v, fo, ho, wo):
    dma = pltpu.SemaphoreType.DMA
    vmem = pl.BlockSpec(memory_space=pltpu.VMEM)
    anywhere = pl.BlockSpec(memory_space=pl.ANY)
    return pl.pallas_call(
        move_kernel,
        out_shape=[jax.ShapeDtypeStruct((2, SPANS, PIECE, HEAD), BF16), jax.ShapeDtypeStruct((SPANS, 2, KEYS, HEAD), BF16),
                   jax.ShapeDtypeStruct((8, HEAD), F32)],
        in_specs=[anywhere] * 7,
        out_specs=[vmem, vmem, vmem],
        scratch_shapes=[pltpu.VMEM((TILE, HEAD), BF16), pltpu.VMEM((TILE, HEAD), BF16), pltpu.VMEM((1, HEAD), F32),
                        pltpu.SMEM((SPANS,), jnp.int32), pltpu.SMEM((SPANS,), jnp.int32), pltpu.SMEM((SPANS,), jnp.int32),
                        dma((7,)), dma((8,)), dma((16,)), dma((3,)), dma((2,)), dma((30,)), dma((16, 2)), dma((16, 2)), dma((16, 2)), dma(())],
        compiler_params=pltpu.CompilerParams(collective_id=0, has_side_effects=True, vmem_limit_bytes=60 << 20),
    )(q, k, v, frequencies(), fo, ho, wo)


def column_to_row(column):
    eye = lax.broadcasted_iota(jnp.int32, column.shape, 0) == lax.broadcasted_iota(jnp.int32, column.shape, 1)
    return jnp.sum(jnp.where(eye, column, 0.0), axis=0, keepdims=True)


def encode(row):
    first = row.astype(BF16).astype(F32)
    second = (row - first).astype(BF16).astype(F32)
    third = (row - first - second).astype(BF16).astype(F32)
    place = lax.broadcasted_iota(jnp.int32, (16, HEAD), 0)
    tile = jnp.where(place == 0, first, jnp.where(place == 1, second, jnp.where(place == 2, third, 0.0)))
    return tile.astype(BF16)


def attend_kernel(table_in, bound, qg, kv, acc, top, table, cells, sem):
    load = pltpu.make_async_copy(table_in, table, sem)
    load.start()
    acc[...] = jnp.zeros_like(acc)
    ones = jnp.ones((KEYS, HEAD), BF16)
    safe = jnp.max(bound[...]) <= LIMIT
    load.wait()
    total = jnp.int32(0)
    for c in range(SPANS):
        for d in range(c + 1):
            cells[total] = c * SPANS + d
            total = total + table[c, d]
    for n in range(UNROLL - 1):
        cells[total + n] = SPANS * SPANS

    def operands(n):
        code = cells[n]
        c = code // SPANS
        d = code % SPANS
        cc = jnp.minimum(c, SPANS - 1)
        q = jnp.concatenate([qg[0, cc], qg[1, cc]], axis=0)
        s = lax.dot_general(q, kv[d, 0], (((1,), (1,)), ((), ())), preferred_element_type=F32)
        return c, s, jnp.concatenate([kv[d, 1], ones], axis=1)

    @pl.when(safe)
    def _():
        top[...] = jnp.zeros_like(top)

        @pl.loop(0, (total + UNROLL - 1) // UNROLL)
        def _(step):
            for u in range(UNROLL):
                c, s, v = operands(step * UNROLL + u)
                p = jnp.exp2(s * SCALE2).astype(BF16)
                acc[c] += jnp.dot(p, v, preferred_element_type=F32)

    @pl.when(jnp.logical_not(safe))
    def _():
        top[...] = jnp.full_like(top, -1e30)

        @pl.loop(0, total)
        def _(n):
            c, s, v = operands(n)
            s = s * SCALE
            old = top[c]
            new = jnp.maximum(old, jnp.max(s, axis=1, keepdims=True))
            p = jnp.exp(s - new[:, 0:1]).astype(BF16)
            shrink = jnp.exp(old - new)
            acc[c] = acc[c] * jnp.concatenate([shrink, shrink], axis=1) + jnp.dot(p, v, preferred_element_type=F32)
            top[c] = new


def attend(table, bound, qg, kv):
    vmem = pl.BlockSpec(memory_space=pltpu.VMEM)
    return pl.pallas_call(
        attend_kernel,
        out_shape=[jax.ShapeDtypeStruct((SPANS + 1, ROWS, 2 * HEAD), F32), jax.ShapeDtypeStruct((SPANS + 1, ROWS, HEAD), F32)],
        in_specs=[pl.BlockSpec(memory_space=pl.ANY), vmem, vmem, vmem],
        out_specs=[vmem, vmem],
        scratch_shapes=[pltpu.SMEM((SPANS, SPANS), jnp.int32), pltpu.SMEM((160,), jnp.int32), pltpu.SemaphoreType.DMA(())],
        compiler_params=pltpu.CompilerParams(vmem_limit_bytes=60 << 20),
    )(table, bound, qg, kv)


def read_rows(block):
    parts = block.astype(F32)
    return parts[0:1] + parts[1:2] + parts[2:3]


def row_to_column(row):
    eye = lax.broadcasted_iota(jnp.int32, (PIECE, HEAD), 0) == lax.broadcasted_iota(jnp.int32, (PIECE, HEAD), 1)
    return jnp.sum(jnp.where(eye, jnp.broadcast_to(row, (PIECE, HEAD)), 0.0), axis=1, keepdims=True)


def merge_kernel(acc, top, out, part, arrived, m_send, m_recv, local_sem):
    qa, kb, z, core = coords()
    home = qa // 8
    slot = qa % 8
    mine = z // 2

    barrier = pltpu.get_barrier_semaphore()

    def goes(n, c):
        half = (z + n) % 2
        return half, (c, (2 * core + half) * 2 + home)

    def stays(n, c):
        half, device = goes(n, c)
        return jnp.logical_and(c == qa, device[1] == kb)

    for i in range(8):
        for zz in range(4):
            device = (8 * core + i, zz * 2 + mine)
            @pl.when(jnp.logical_or(device[0] != qa, device[1] != kb))
            def _():
                pl.semaphore_signal(barrier, inc=1, device_id=device, device_id_type=MESH)

    for c in range(SPANS):
        for half in range(2):
            rows = pl.ds(half * PIECE, PIECE)
            sums = acc[c, rows, HEAD:]
            part[half, c, 0:PIECE] = (acc[c, rows, :HEAD] / sums).astype(BF16)
            part[half, c, PIECE:] = encode(column_to_row(jnp.log(sums) + top[c, rows]))
    own = jnp.where(jnp.logical_and(home == core, mine == core), 1, 0)
    pl.semaphore_wait(barrier, 32 - own)

    def give(n, c):
        half, device = goes(n, c)
        return remote(part.at[half, c], arrived.at[slot, z], m_send.at[n, c], m_recv.at[slot, z], device)

    for c in range(SPANS):
        for n in range(2):
            @pl.when(jnp.logical_not(stays(n, c)))
            def _():
                give(n, c).start()

            @pl.when(stays(n, c))
            def _():
                keep = pltpu.make_async_copy(part.at[goes(n, c)[0], c], arrived.at[slot, z], local_sem)
                keep.start()
                keep.wait()

    for i in range(8):
        for zz in range(4):
            device = (8 * core + i, zz * 2 + mine)
            @pl.when(jnp.logical_or(device[0] != qa, device[1] != kb))
            def _():
                remote(part.at[0, 0], arrived.at[i, zz], m_send.at[0, 0], m_recv.at[i, zz], device).wait_recv()
    for i in range(8):
        levels = [read_rows(arrived[i, zz, PIECE:]) for zz in range(4)]
        peak = jnp.maximum(jnp.maximum(levels[0], levels[1]), jnp.maximum(levels[2], levels[3]))
        weights = [jnp.exp(level - peak) for level in levels]
        total = weights[0] + weights[1] + weights[2] + weights[3]
        value = None
        for zz in range(4):
            term = row_to_column(weights[zz] / total) * arrived[i, zz, 0:PIECE].astype(F32)
            value = term if value is None else value + term
        out[STARTS[i]:STARTS[i] + PIECE] = value.astype(BF16)

    for c in range(SPANS):
        for n in range(2):
            @pl.when(jnp.logical_not(stays(n, c)))
            def _():
                give(n, c).wait_send()


def merge(acc, top):
    dma = pltpu.SemaphoreType.DMA
    vmem = pl.BlockSpec(memory_space=pltpu.VMEM)
    block = (PIECE + 16, HEAD)
    return pl.pallas_call(
        merge_kernel,
        out_shape=jax.ShapeDtypeStruct((TILE, HEAD), BF16),
        in_specs=[vmem, vmem],
        out_specs=vmem,
        scratch_shapes=[pltpu.VMEM((2, SPANS) + block, BF16), pltpu.VMEM((8, 4) + block, BF16),
                        dma((2, SPANS)), dma((8, 4)), dma(())],
        compiler_params=pltpu.CompilerParams(collective_id=1, has_side_effects=True, vmem_limit_bytes=60 << 20),
    )(acc, top)


def local(q, k, v, table, fo, ho, wo):
    qg, kv, bound = move(q, k, v, fo, ho, wo)
    return merge(*attend(table, bound, qg, kv))


def solution(mesh):
    rows = P(("qa", "kb"), None)
    return jax.shard_map(local, mesh=mesh, in_specs=(rows, rows, rows, P(), P(), P(), P()), out_specs=rows, check_vma=False)
```

```python
import jax
import jax.numpy as jnp
import numpy as np
from jax import lax
from jax.experimental import pallas as pl
from jax.experimental.pallas import tpu as pltpu
from jax.sharding import PartitionSpec as P

HEIGHT = 32
WIDTH = 52
SPANS = 16
TILE = 624
HEAD = 128
PIECE = 80
STARTS = tuple(16 * (i * 34 // 7) for i in range(8))
MESH = pl.DeviceIdType.MESH
BF16 = jnp.bfloat16
F32 = jnp.float32
ROWS = 2 * PIECE
KEYS = 2 * TILE
UNROLL = 4
SCALE = float(HEAD ** -0.5)
SCALE2 = float(HEAD ** -0.5 * np.log2(np.e))
LOWEST = 1e-25
HIGHEST = 1e30


def coords():
    qa = lax.axis_index("qa")
    kb = lax.axis_index("kb")
    return qa, kb, kb // 2, kb % 2


def turn_table(freq_ref, numbers, qa, kb):
    row = lax.broadcasted_iota(jnp.int32, (TILE, HEAD), 0)
    lane = lax.broadcasted_iota(jnp.int32, (TILE, HEAD), 1) % 64
    within = (row + kb * TILE).astype(F32)
    frame = jnp.floor((within + 0.5) * (1.0 / (HEIGHT * WIDTH)))
    line = jnp.floor((within + 0.5) * (1.0 / WIDTH))
    column = within - line * WIDTH + numbers[SPANS + 2, qa].astype(F32)
    line = line - frame * HEIGHT + numbers[SPANS + 1, qa].astype(F32)
    frame = frame + numbers[SPANS, qa].astype(F32)
    angles = jnp.where(lane < 22, frame, jnp.where(lane < 43, line, column)) * freq_ref[...]
    turns = jnp.floor(angles * np.float32(2 / np.pi) + 0.5)
    rest = angles - turns * np.float32(1.5703125)
    rest = rest - turns * np.float32(4.837512969970703125e-4)
    rest = rest - turns * np.float32(7.54978995489188216e-8)
    sq = rest * rest
    sine = rest + rest * sq * (np.float32(-1 / 6) + sq * (np.float32(8.3333333e-3) + sq * (np.float32(-1.98412698e-4) + sq * np.float32(2.7525562e-6))))
    cosine = 1.0 + sq * (np.float32(-0.5) + sq * (np.float32(4.16666667e-2) + sq * (np.float32(-1.38888889e-3) + sq * (np.float32(2.48015873e-5) + sq * np.float32(-2.7557319e-7)))))
    half = jnp.floor(turns * 0.5)
    odd = (turns - 2.0 * half) > 0.5
    flip = (half - 2.0 * jnp.floor(half * 0.5)) > 0.5
    sign = jnp.where(flip, -1.0, 1.0)
    cos_out = jnp.where(odd, -sine, cosine) * sign
    sin_out = jnp.where(odd, cosine, sine) * sign
    full_lane = lax.broadcasted_iota(jnp.int32, (TILE, HEAD), 1)
    return cos_out, jnp.where(full_lane < 64, -sin_out, sin_out)


def turn(rows, cos_out, sin_out):
    x = rows.astype(F32)
    return (x * cos_out + pltpu.roll(x, 64, 1) * sin_out).astype(BF16)


NEAR = ((0, 0), (3, 0), (0, 3), (1, 0), (0, 1), (2, 0), (0, 2))
EARLY = 24
FIRST = (1, 1, 1, 1, 1)


def near_order(core):
    return [(jnp.where(core == 0, j, i), jnp.where(core == 0, i, j)) for i, j in NEAR]


def remote(src, dst, send, recv, device):
    return pltpu.make_async_remote_copy(src_ref=src, dst_ref=dst, send_sem=send, recv_sem=recv, device_id=device, device_id_type=MESH)


def move_kernel(rows_in, freq, numbers_in, qg, kv, acc,
                qs, numbers, in_sem, q_send, q_recv, z_send, z_recv, kv_send, kv_recv, t_send, t_recv):
    qa, kb, z, core = coords()
    step_a = 1 + 3 * core
    step_b = 4 - 3 * core
    a = (qa // step_a) % 4
    b = (qa // step_b) % 4
    entry = z // 2 == core
    twin = (qa, z * 2 + 1 - core)
    mine = pl.ds(core * TILE, TILE)

    def at(aa, bb):
        return (aa % 4) * step_a + (bb % 4) * step_b

    barrier = pltpu.get_barrier_semaphore()
    loads = [pltpu.make_async_copy(numbers_in, numbers, in_sem.at[0]),
             pltpu.make_async_copy(rows_in.at[2], kv.at[qa, 1, mine], in_sem.at[1])]
    for load in loads:
        load.start()
    for device in ((at(a + 1, b), kb), (at(a + 3, b), kb), (at(a, b + 1), kb), (at(a, b + 3), kb), twin):
        pl.semaphore_signal(barrier, inc=1, device_id=device, device_id_type=MESH)

    q_home = z * 2 + qa // 8

    @pl.when(entry)
    def _():
        for c in range(SPANS):
            @pl.when(jnp.logical_or(c != qa, q_home != kb))
            def _():
                pl.semaphore_signal(barrier, inc=1, device_id=(c, q_home), device_id_type=MESH)
    for half in range(2):
        @pl.when(2 * core + half != z)
        def _():
            pl.semaphore_signal(barrier, inc=1, device_id=(qa, (2 * core + half) * 2 + core), device_id_type=MESH)
    acc[...] = jnp.zeros_like(acc)
    for load in loads:
        load.wait()
    cos_out, sin_out = turn_table(freq, numbers, qa, kb)
    qs[...] = turn(rows_in[0], cos_out, sin_out)
    kv[qa, 0, mine] = turn(rows_in[1], cos_out, sin_out)
    greeted = 13 + jnp.where(entry, 3, 0) - jnp.where(jnp.logical_and(entry, qa // 8 == core), 1, 0)
    pl.semaphore_wait(barrier, greeted)

    def q_copy(t):
        i = (qa + t) % 8
        rows = pl.ds(pl.multiple_of(16 * (i * 34 // 7), 16), PIECE)
        return rows, remote(qs.at[rows], qg.at[z % 2, qa], q_send, q_recv, (8 * core + i, z * 2 + z // 2))

    to_me = jnp.logical_and(qa // 8 == core, entry)
    for t in range(1, 8):
        q_copy(t)[1].start()

    @pl.when(jnp.logical_not(to_me))
    def _():
        q_copy(0)[1].start()

    @pl.when(to_me)
    def _():
        pltpu.make_async_copy(qs.at[q_copy(0)[0]], qg.at[z % 2, qa], q_recv).start()


    def part_ref(span, part):
        return kv.at[span, part, mine]

    def kv_copy(span, part, device):
        copy = remote(part_ref(span, part), part_ref(span, part), kv_send, kv_recv.at[span, part], device)
        copy.start()

    def kv_wait(span, part):
        remote(part_ref(span, part), part_ref(span, part), kv_send, kv_recv.at[span, part], twin).wait_recv()

    def slot_of(span):
        return span

    def twin_copy(span):
        ref = kv.at[span, :, mine]
        return remote(ref, ref, t_send, t_recv.at[slot_of(span)], twin)

    def twin_wait(span):
        ref = kv.at[span, :, pl.ds((1 - core) * TILE, TILE)]
        remote(ref, ref, t_send, t_recv.at[slot_of(span)], twin).wait_recv()

    up_a, down_a = (at(a + 1, b), kb), (at(a - 1, b), kb)
    up_b, down_b = (at(a, b + 1), kb), (at(a, b - 1), kb)
    for part in (1, 0):
        for device in (up_a, down_a, up_b, down_b):
            kv_copy(qa, part, device)
    twin_copy(qa).start()

    def z_copy(d):
        return remote(qg.at[z % 2], qg.at[z % 2], z_send.at[d - 1], z_recv.at[z % 2], (qa, (kb + 2 * d) % 8))

    @pl.when(entry)
    def _():
        remote(qg.at[z % 2], qg.at[z % 2], q_send, q_recv, twin).wait_recv()
        for d in (2, 1, 3):
            z_copy(d).start()

    def arrive(span, part, devices):
        kv_wait(span, part)
        for device in devices:
            kv_copy(span, part, device)
        if part == 0:
            twin_copy(span).start()

    arrive(at(a - 1, b), 1, (up_a, up_b, down_b))
    arrive(at(a + 1, b), 1, (up_b, down_b))
    arrive(at(a, b - 1), 1, (up_b,))
    arrive(at(a, b + 1), 1, ())
    arrive(at(a - 1, b), 0, (up_b, down_b))
    arrive(at(a + 1, b), 0, (down_a, up_b, down_b))
    arrive(at(a, b - 1), 0, ())
    arrive(at(a, b + 1), 0, (down_b,))
    arrive(at(a + 2, b), 1, (up_b, down_b))
    arrive(at(a + 2, b), 0, (up_b, down_b))
    ones = jnp.ones((KEYS, HEAD), BF16)

    spans = [at(a + i, b + j) for i, j in near_order(core)]
    begins = [jnp.int32(0)]
    for span in spans:
        begins.append(begins[-1] + SPANS - span)

    def cells(n):
        for u in range(UNROLL):
            t = n + u
            d = spans[0]
            c = d + t
            for span, begin in zip(spans[1:], begins[1:]):
                here = t >= begin
                d = jnp.where(here, span, d)
                c = jnp.where(here, span + t - begin, c)
            cc = jnp.minimum(c, SPANS - 1)
            weight = jnp.where(t < begins[-1], numbers[cc, d], 0).astype(F32)
            q = jnp.concatenate([qg[0, cc], qg[1, cc]], axis=0)
            scores = lax.dot_general(q, kv[d, 0], (((1,), (1,)), ((), ())), preferred_element_type=F32)
            p = jnp.exp2(scores * SCALE2).astype(BF16)
            v = jnp.concatenate([kv[d, 1], ones], axis=1)
            acc[cc] += weight * jnp.dot(p, v, preferred_element_type=F32)

    arrive(at(a, b + 2), 1, ())
    arrive(at(a, b + 2), 0, ())
    done = [0]

    def next_cells(n):
        start = done[0]
        done[0] = min(EARLY // UNROLL, start + n)

        @pl.loop(start, done[0])
        def _(step):
            cells(step * UNROLL)

    def events(step, middle, last):
        arrive(at(a + step, b - 1), 1, (up_b,))
        arrive(at(a + step, b + 1), 1, ())
        next_cells(middle)
        arrive(at(a + step, b - 1), 0, ())
        arrive(at(a + step, b + 1), 0, (down_b,))
        next_cells(last)

    events(3, 0, 0)
    for half in range(2):
        @pl.when(jnp.logical_or(jnp.logical_not(entry), half != z % 2))
        def _():
            remote(qg.at[half], qg.at[half], z_send.at[0], z_recv.at[half], twin).wait_recv()
    for i, j in NEAR:
        twin_wait(at(a + i, b + j))
    next_cells(FIRST[0])
    events(1, FIRST[1], FIRST[2])
    events(2, FIRST[3], FIRST[4])
    next_cells(EARLY)
    for step in (3, 1, 2):
        arrive(at(a + step, b + 2), 1, ())
        arrive(at(a + step, b + 2), 0, ())
    for i in (0, 3, 1, 2):
        for j in (0, 3, 1, 2):
            if (i, j) not in NEAR:
                twin_wait(at(a + i, b + j))

    @pl.when(entry)
    def _():
        for d in (1, 2, 3):
            z_copy(d).wait_send()
    @pl.when(to_me)
    def _():
        remote(qg.at[0, pl.ds(0, 7)], qg.at[0, pl.ds(0, 7)], q_send, q_recv, twin).wait_send()

    @pl.when(jnp.logical_not(to_me))
    def _():
        remote(qg.at[0, pl.ds(0, 8)], qg.at[0, pl.ds(0, 8)], q_send, q_recv, twin).wait_send()
    ref = kv.at[pl.ds(0, 15), :, mine]
    remote(ref, ref, kv_send, kv_recv.at[0, 0], twin).wait_send()
    ref = kv.at[:, :, mine]
    remote(ref, ref, t_send, t_recv.at[0], twin).wait_send()


def frequencies():
    lead = 1.0 / 10000.0 ** (np.arange(22, dtype=np.float32) / np.float32(22))
    side = 1.0 / 10000.0 ** (np.arange(21, dtype=np.float32) / np.float32(21))
    one = np.concatenate([lead, side, side]).astype(np.float32)
    return jnp.asarray(np.concatenate([one, one])[None])


def move(rows, numbers):
    dma = pltpu.SemaphoreType.DMA
    vmem = pl.BlockSpec(memory_space=pltpu.VMEM)
    anywhere = pl.BlockSpec(memory_space=pl.ANY)
    return pl.pallas_call(
        move_kernel,
        out_shape=[jax.ShapeDtypeStruct((2, SPANS, PIECE, HEAD), BF16), jax.ShapeDtypeStruct((SPANS, 2, KEYS, HEAD), BF16),
                   jax.ShapeDtypeStruct((SPANS, ROWS, 2 * HEAD), F32)],
        in_specs=[vmem, vmem, anywhere],
        out_specs=[vmem] * 3,
        scratch_shapes=[pltpu.VMEM((TILE, HEAD), BF16), pltpu.SMEM((SPANS + 3, SPANS), jnp.int32),
                        dma((2,)), dma(()), dma(()), dma((3,)), dma((2,)), dma(()), dma((16, 2)), dma(()), dma((16,))],
        compiler_params=pltpu.CompilerParams(collective_id=0, has_side_effects=True, vmem_limit_bytes=24 << 20),
    )(rows, frequencies(), numbers)


def column_to_row(column):
    eye = lax.broadcasted_iota(jnp.int32, column.shape, 0) == lax.broadcasted_iota(jnp.int32, column.shape, 1)
    return jnp.sum(jnp.where(eye, column, 0.0), axis=0, keepdims=True)


def encode(row):
    first = row.astype(BF16).astype(F32)
    second = (row - first).astype(BF16).astype(F32)
    third = (row - first - second).astype(BF16).astype(F32)
    place = lax.broadcasted_iota(jnp.int32, (16, HEAD), 0)
    tile = jnp.where(place == 0, first, jnp.where(place == 1, second, jnp.where(place == 2, third, 0.0)))
    return tile.astype(BF16)


def attend_kernel(table_in, qg, kv, begun, acc, top, table, cells, keep, sem):
    load = pltpu.make_async_copy(table_in, table, sem)
    load.start()
    acc[:SPANS] = begun[...]
    acc[SPANS] = jnp.zeros((ROWS, 2 * HEAD), F32)
    ones = jnp.ones((KEYS, HEAD), BF16)
    qa = lax.axis_index("qa")
    for d in range(SPANS):
        keep[d] = jnp.int32(EARLY)
    begin = jnp.int32(0)
    for i, j in NEAR:
        d = (qa // 4 + i) % 4 * 4 + (qa + j) % 4
        keep[d] = begin
        begin = begin + SPANS - d
    load.wait()

    def gather(skip):
        total = jnp.int32(0)
        for c in range(SPANS):
            for d in range(c + 1):
                cells[total] = c * SPANS + d
                allowed = table[c, d]
                total = total + (jnp.where(keep[d] + (c - d) >= EARLY, allowed, 0) if skip else allowed)
        for n in range(UNROLL - 1):
            cells[total + n] = SPANS * SPANS
        return total

    def operands(n):
        code = cells[n]
        c = code // SPANS
        d = code % SPANS
        cc = jnp.minimum(c, SPANS - 1)
        q = jnp.concatenate([qg[0, cc], qg[1, cc]], axis=0)
        s = lax.dot_general(q, kv[d, 0], (((1,), (1,)), ((), ())), preferred_element_type=F32)
        return c, s, jnp.concatenate([kv[d, 1], ones], axis=1)

    top[...] = jnp.zeros_like(top)
    total = gather(True)

    @pl.loop(0, (total + UNROLL - 1) // UNROLL)
    def _(step):
        for u in range(UNROLL):
            c, s, v = operands(step * UNROLL + u)
            p = jnp.exp2(s * SCALE2).astype(BF16)
            acc[c] += jnp.dot(p, v, preferred_element_type=F32)

    sums = acc[:SPANS, :, HEAD:]
    good = jnp.where(jnp.logical_and(sums >= LOWEST, sums <= HIGHEST), 1.0, 0.0)

    @pl.when(jnp.min(good) < 0.5)
    def _():
        top[...] = jnp.full_like(top, -1e30)
        acc[...] = jnp.zeros_like(acc)
        total = gather(False)

        @pl.loop(0, total)
        def _(n):
            c, s, v = operands(n)
            s = s * SCALE
            old = top[c]
            new = jnp.maximum(old, jnp.max(s, axis=1, keepdims=True))
            p = jnp.exp(s - new[:, 0:1]).astype(BF16)
            shrink = jnp.exp(old - new)
            acc[c] = acc[c] * jnp.concatenate([shrink, shrink], axis=1) + jnp.dot(p, v, preferred_element_type=F32)
            top[c] = new


def attend(table, qg, kv, begun):
    vmem = pl.BlockSpec(memory_space=pltpu.VMEM)
    return pl.pallas_call(
        attend_kernel,
        out_shape=[jax.ShapeDtypeStruct((SPANS + 1, ROWS, 2 * HEAD), F32), jax.ShapeDtypeStruct((SPANS + 1, ROWS, HEAD), F32)],
        in_specs=[pl.BlockSpec(memory_space=pl.ANY), vmem, vmem, vmem],
        out_specs=[vmem, vmem],
        scratch_shapes=[pltpu.SMEM((SPANS + 3, SPANS), jnp.int32), pltpu.SMEM((160,), jnp.int32), pltpu.SMEM((SPANS,), jnp.int32), pltpu.SemaphoreType.DMA(())],
        compiler_params=pltpu.CompilerParams(vmem_limit_bytes=24 << 20),
    )(table, qg, kv, begun)


def read_rows(block):
    parts = block.astype(F32)
    return parts[0:1] + parts[1:2] + parts[2:3]


def row_to_column(row):
    eye = lax.broadcasted_iota(jnp.int32, (PIECE, HEAD), 0) == lax.broadcasted_iota(jnp.int32, (PIECE, HEAD), 1)
    return jnp.sum(jnp.where(eye, jnp.broadcast_to(row, (PIECE, HEAD)), 0.0), axis=1, keepdims=True)


def merge_kernel(acc, top, out, part, arrived, m_send, m_recv):
    qa, kb, z, core = coords()
    home = qa // 8
    slot = qa % 8
    mine = z // 2

    barrier = pltpu.get_barrier_semaphore()

    own = jnp.logical_and(home == core, mine == core)
    for t in range(8):
        for n in range(4):
            device = (8 * core + (qa + t) % 8, (z + n) % 4 * 2 + mine)
            if t or n:
                pl.semaphore_signal(barrier, inc=1, device_id=device, device_id_type=MESH)
            else:
                @pl.when(jnp.logical_not(own))
                def _():
                    pl.semaphore_signal(barrier, inc=1, device_id=device, device_id_type=MESH)

    def finish(t):
        c = (qa + t) % SPANS
        for half in range(2):
            rows = pl.ds(half * PIECE, PIECE)
            sums = acc[c, rows, HEAD:]
            part[half, c, 0:PIECE] = (acc[c, rows, :HEAD] / sums).astype(BF16)
            part[half, c, PIECE:] = encode(column_to_row(jnp.log(sums) + top[c, rows]))

    def give(t, n):
        c = (qa + t) % SPANS
        half = (z + n) % 2
        return half, c, remote(part.at[half, c], arrived.at[slot, z], m_send, m_recv, (c, (2 * core + half) * 2 + home))

    def send(t):
        for n in range(2):
            half, c, copy = give(t, n)
            if t or n:
                copy.start()
            else:
                @pl.when(own)
                def _():
                    pltpu.make_async_copy(part.at[half, c], arrived.at[slot, z], m_recv).start()

                @pl.when(jnp.logical_not(own))
                def _():
                    copy.start()

    for t in range(8):
        finish(t)
    pl.semaphore_wait(barrier, 32 - jnp.where(own, 1, 0))
    for t in range(8):
        send(t)
    for block in range(2):
        for t in range(8 + 4 * block, 12 + 4 * block):
            finish(t)
        for t in range(8 + 4 * block, 12 + 4 * block):
            send(t)

    remote(arrived, arrived, m_send, m_recv, (qa, kb)).wait_recv()
    for i in range(8):
        levels = [read_rows(arrived[i, zz, PIECE:]) for zz in range(4)]
        peak = jnp.maximum(jnp.maximum(levels[0], levels[1]), jnp.maximum(levels[2], levels[3]))
        weights = [jnp.exp(level - peak) for level in levels]
        total = weights[0] + weights[1] + weights[2] + weights[3]
        value = None
        for zz in range(4):
            term = row_to_column(weights[zz] / total) * arrived[i, zz, 0:PIECE].astype(F32)
            value = term if value is None else value + term
        out[STARTS[i]:STARTS[i] + PIECE] = value.astype(BF16)

    every = part.at[:]

    @pl.when(own)
    def _():
        remote(part.at[0, pl.ds(1, 15)], part.at[0, pl.ds(1, 15)], m_send, m_recv, (qa, kb)).wait_send()
        remote(part.at[1], part.at[1], m_send, m_recv, (qa, kb)).wait_send()

    @pl.when(jnp.logical_not(own))
    def _():
        remote(every, every, m_send, m_recv, (qa, kb)).wait_send()


def merge(acc, top):
    dma = pltpu.SemaphoreType.DMA
    vmem = pl.BlockSpec(memory_space=pltpu.VMEM)
    block = (PIECE + 16, HEAD)
    return pl.pallas_call(
        merge_kernel,
        out_shape=jax.ShapeDtypeStruct((TILE, HEAD), BF16),
        in_specs=[vmem, vmem],
        out_specs=vmem,
        scratch_shapes=[pltpu.VMEM((2, SPANS) + block, BF16), pltpu.VMEM((8, 4) + block, BF16),
                        dma(()), dma(())],
        compiler_params=pltpu.CompilerParams(collective_id=1, has_side_effects=True, vmem_limit_bytes=24 << 20),
    )(acc, top)


def local(q, k, v, table, fo, ho, wo):
    rows = jnp.stack([q, k, v])
    numbers = jnp.concatenate([table, fo[None], ho[None], wo[None]])
    qg, kv, begun = move(rows, numbers)
    return merge(*attend(numbers, qg, kv, begun))


def solution(mesh):
    rows = P(("qa", "kb"), None)
    return jax.shard_map(local, mesh=mesh, in_specs=(rows, rows, rows, P(), P(), P(), P()), out_specs=rows, check_vma=False)
```

```python
import jax
import jax.numpy as jnp
import numpy as np
from jax import lax
from jax.experimental import pallas as pl
from jax.experimental.pallas import tpu as pltpu
from jax.sharding import PartitionSpec as P

HEIGHT = 32
WIDTH = 52
SPANS = 16
TILE = 624
HEAD = 128
PIECE = 80
STARTS = tuple(16 * (i * 34 // 7) for i in range(8))
MESH = pl.DeviceIdType.MESH
BF16 = jnp.bfloat16
F32 = jnp.float32
ROWS = 2 * PIECE
KEYS = 2 * TILE
UNROLL = 4
SCALE = float(HEAD ** -0.5)
SCALE2 = float(HEAD ** -0.5 * np.log2(np.e))
LOWEST = 1e-25
HIGHEST = 1e30


def coords():
    qa = lax.axis_index("qa")
    kb = lax.axis_index("kb")
    return qa, kb, kb // 2, kb % 2


def turn_table(numbers, qa, kb):
    row = lax.broadcasted_iota(jnp.int32, (TILE, HEAD), 0)
    lane = lax.broadcasted_iota(jnp.int32, (TILE, HEAD), 1) % 64
    within = (row + kb * TILE).astype(F32)
    frame = jnp.floor((within + 0.5) * (1.0 / (HEIGHT * WIDTH)))
    line = jnp.floor((within + 0.5) * (1.0 / WIDTH))
    column = within - line * WIDTH + numbers[SPANS + 2, qa].astype(F32)
    line = line - frame * HEIGHT + numbers[SPANS + 1, qa].astype(F32)
    frame = frame + numbers[SPANS, qa].astype(F32)
    angles = jnp.where(lane < 22, frame, jnp.where(lane < 43, line, column)) * frequencies()
    turns = jnp.floor(angles * np.float32(2 / np.pi) + 0.5)
    rest = angles - turns * np.float32(1.5703125)
    rest = rest - turns * np.float32(4.837512969970703125e-4)
    rest = rest - turns * np.float32(7.54978995489188216e-8)
    sq = rest * rest
    sine = rest + rest * sq * (np.float32(-1 / 6) + sq * (np.float32(8.3333333e-3) + sq * (np.float32(-1.98412698e-4) + sq * np.float32(2.7525562e-6))))
    cosine = 1.0 + sq * (np.float32(-0.5) + sq * (np.float32(4.16666667e-2) + sq * (np.float32(-1.38888889e-3) + sq * (np.float32(2.48015873e-5) + sq * np.float32(-2.7557319e-7)))))
    half = jnp.floor(turns * 0.5)
    odd = (turns - 2.0 * half) > 0.5
    flip = (half - 2.0 * jnp.floor(half * 0.5)) > 0.5
    sign = jnp.where(flip, -1.0, 1.0)
    cos_out = jnp.where(odd, -sine, cosine) * sign
    sin_out = jnp.where(odd, cosine, sine) * sign
    full_lane = lax.broadcasted_iota(jnp.int32, (TILE, HEAD), 1)
    return cos_out, jnp.where(full_lane < 64, -sin_out, sin_out)


def turn(rows, cos_out, sin_out):
    x = rows.astype(F32)
    return (x * cos_out + pltpu.roll(x, 64, 1) * sin_out).astype(BF16)


NEAR = ((0, 0), (3, 0), (0, 3), (1, 0), (0, 1), (2, 0), (0, 2))
EARLY = 28
SLOTS = (0, 1, 1, 1, 1, 1, 1, 1)


def near_order(core):
    return [(jnp.where(core == 0, j, i), jnp.where(core == 0, i, j)) for i, j in NEAR]


def remote(src, dst, send, recv, device):
    return pltpu.make_async_remote_copy(src_ref=src, dst_ref=dst, send_sem=send, recv_sem=recv, device_id=device, device_id_type=MESH)


def move_kernel(rows_in, numbers_in, qg, kv, acc,
                qs, numbers, in_sem, q_send, q_recv, z_send, z_recv, kv_send, kv_recv, t_send, t_recv):
    qa, kb, z, core = coords()
    step_a = 1 + 3 * core
    step_b = 4 - 3 * core
    a = (qa // step_a) % 4
    b = (qa // step_b) % 4
    entry = z // 2 == core
    twin = (qa, z * 2 + 1 - core)
    mine = pl.ds(core * TILE, TILE)

    def at(aa, bb):
        return (aa % 4) * step_a + (bb % 4) * step_b

    barrier = pltpu.get_barrier_semaphore()
    loads = [pltpu.make_async_copy(numbers_in, numbers, in_sem.at[0]),
             pltpu.make_async_copy(rows_in.at[2], kv.at[qa, 1, mine], in_sem.at[1])]
    for load in loads:
        load.start()
    for device in ((at(a + 1, b), kb), (at(a + 3, b), kb), (at(a, b + 1), kb), (at(a, b + 3), kb), twin):
        pl.semaphore_signal(barrier, inc=1, device_id=device, device_id_type=MESH)

    q_home = z * 2 + qa // 8

    @pl.when(entry)
    def _():
        for c in range(SPANS):
            @pl.when(jnp.logical_or(c != qa, q_home != kb))
            def _():
                pl.semaphore_signal(barrier, inc=1, device_id=(c, q_home), device_id_type=MESH)
    for half in range(2):
        @pl.when(2 * core + half != z)
        def _():
            pl.semaphore_signal(barrier, inc=1, device_id=(qa, (2 * core + half) * 2 + core), device_id_type=MESH)
    acc[...] = jnp.zeros_like(acc)
    for load in loads:
        load.wait()
    cos_out, sin_out = turn_table(numbers, qa, kb)
    qs[...] = turn(rows_in[0], cos_out, sin_out)
    kv[qa, 0, mine] = turn(rows_in[1], cos_out, sin_out)
    greeted = 13 + jnp.where(entry, 3, 0) - jnp.where(jnp.logical_and(entry, qa // 8 == core), 1, 0)
    pl.semaphore_wait(barrier, greeted)

    def q_copy(t):
        i = (qa + t) % 8
        rows = pl.ds(pl.multiple_of(16 * (i * 34 // 7), 16), PIECE)
        return rows, remote(qs.at[rows], qg.at[z % 2, qa], q_send, q_recv, (8 * core + i, z * 2 + z // 2))

    to_me = jnp.logical_and(qa // 8 == core, entry)
    for t in range(1, 8):
        q_copy(t)[1].start()

    @pl.when(jnp.logical_not(to_me))
    def _():
        q_copy(0)[1].start()

    @pl.when(to_me)
    def _():
        pltpu.make_async_copy(qs.at[q_copy(0)[0]], qg.at[z % 2, qa], q_recv).start()


    def part_ref(span, part):
        return kv.at[span, part, mine]

    def kv_copy(span, part, device):
        copy = remote(part_ref(span, part), part_ref(span, part), kv_send, kv_recv.at[span, part], device)
        copy.start()

    def kv_wait(span, part):
        remote(part_ref(span, part), part_ref(span, part), kv_send, kv_recv.at[span, part], twin).wait_recv()

    def slot_of(span):
        return span

    def twin_copy(span):
        ref = kv.at[span, :, mine]
        return remote(ref, ref, t_send, t_recv.at[slot_of(span)], twin)

    def twin_wait(span):
        ref = kv.at[span, :, pl.ds((1 - core) * TILE, TILE)]
        remote(ref, ref, t_send, t_recv.at[slot_of(span)], twin).wait_recv()

    up_a, down_a = (at(a + 1, b), kb), (at(a - 1, b), kb)
    up_b, down_b = (at(a, b + 1), kb), (at(a, b - 1), kb)
    for part in (1, 0):
        for device in (up_a, down_a, up_b, down_b):
            kv_copy(qa, part, device)
    twin_copy(qa).start()

    def z_copy(d):
        return remote(qg.at[z % 2], qg.at[z % 2], z_send.at[d - 1], z_recv.at[z % 2], (qa, (kb + 2 * d) % 8))

    @pl.when(entry)
    def _():
        remote(qg.at[z % 2], qg.at[z % 2], q_send, q_recv, twin).wait_recv()
        for d in (2, 1, 3):
            z_copy(d).start()

    def arrive(span, part, devices):
        kv_wait(span, part)
        for device in devices:
            kv_copy(span, part, device)
        if part == 0:
            twin_copy(span).start()

    arrive(at(a - 1, b), 1, (up_a, up_b, down_b))
    arrive(at(a + 1, b), 1, (up_b, down_b))
    arrive(at(a, b - 1), 1, (up_b,))
    arrive(at(a, b + 1), 1, ())
    arrive(at(a - 1, b), 0, (up_b, down_b))
    arrive(at(a + 1, b), 0, (down_a, up_b, down_b))
    arrive(at(a, b - 1), 0, ())
    arrive(at(a, b + 1), 0, (down_b,))
    arrive(at(a + 2, b), 1, (up_b, down_b))
    arrive(at(a + 2, b), 0, (up_b, down_b))
    ones = jnp.ones((KEYS, HEAD), BF16)

    spans = [at(a + i, b + j) for i, j in near_order(core)]
    begins = [jnp.int32(0)]
    for span in spans:
        begins.append(begins[-1] + SPANS - span)

    def cells(n):
        for u in range(UNROLL):
            t = n + u
            d = spans[0]
            c = d + t
            for span, begin in zip(spans[1:], begins[1:]):
                here = t >= begin
                d = jnp.where(here, span, d)
                c = jnp.where(here, span + t - begin, c)
            cc = jnp.minimum(c, SPANS - 1)
            weight = jnp.where(t < begins[-1], numbers[cc, d], 0).astype(F32)
            q = jnp.concatenate([qg[0, cc], qg[1, cc]], axis=0)
            scores = lax.dot_general(q, kv[d, 0], (((1,), (1,)), ((), ())), preferred_element_type=F32)
            p = jnp.exp2(scores * SCALE2).astype(BF16)
            v = jnp.concatenate([kv[d, 1], ones], axis=1)
            acc[cc] += weight * jnp.dot(p, v, preferred_element_type=F32)

    arrive(at(a, b + 2), 1, ())
    arrive(at(a, b + 2), 0, ())
    done = [0]

    def next_cells(n):
        start = done[0]
        done[0] = min(EARLY // UNROLL, start + n)

        @pl.loop(start, done[0])
        def _(step):
            cells(step * UNROLL)

    def events(step, middle, last):
        arrive(at(a + step, b - 1), 1, (up_b,))
        arrive(at(a + step, b + 1), 1, ())
        next_cells(middle)
        arrive(at(a + step, b - 1), 0, ())
        arrive(at(a + step, b + 1), 0, (down_b,))
        next_cells(last)

    events(3, 0, 0)
    for half in range(2):
        @pl.when(jnp.logical_or(jnp.logical_not(entry), half != z % 2))
        def _():
            remote(qg.at[half], qg.at[half], z_send.at[0], z_recv.at[half], twin).wait_recv()
    for i, j in NEAR:
        twin_wait(at(a + i, b + j))
    next_cells(SLOTS[0])
    events(1, SLOTS[1], SLOTS[2])
    events(2, SLOTS[3], SLOTS[4])
    for step, slot in ((3, 5), (1, 6), (2, 7)):
        next_cells(SLOTS[slot])
        arrive(at(a + step, b + 2), 1, ())
        arrive(at(a + step, b + 2), 0, ())
    for i in (0, 3, 1, 2):
        for j in (0, 3, 1, 2):
            if (i, j) not in NEAR:
                twin_wait(at(a + i, b + j))

    @pl.when(entry)
    def _():
        for d in (1, 2, 3):
            z_copy(d).wait_send()
    @pl.when(to_me)
    def _():
        remote(qg.at[0, pl.ds(0, 7)], qg.at[0, pl.ds(0, 7)], q_send, q_recv, twin).wait_send()

    @pl.when(jnp.logical_not(to_me))
    def _():
        remote(qg.at[0, pl.ds(0, 8)], qg.at[0, pl.ds(0, 8)], q_send, q_recv, twin).wait_send()
    ref = kv.at[pl.ds(0, 15), :, mine]
    remote(ref, ref, kv_send, kv_recv.at[0, 0], twin).wait_send()
    ref = kv.at[:, :, mine]
    remote(ref, ref, t_send, t_recv.at[0], twin).wait_send()


def frequencies():
    lead = 1.0 / 10000.0 ** (np.arange(22, dtype=np.float32) / np.float32(22))
    side = 1.0 / 10000.0 ** (np.arange(21, dtype=np.float32) / np.float32(21))
    lane = lax.broadcasted_iota(jnp.int32, (1, HEAD), 1) % 64
    row = jnp.zeros((1, HEAD), F32)
    for n, value in enumerate(np.concatenate([lead, side, side])):
        row = jnp.where(lane == n, np.float32(value), row)
    return row


def move(rows, numbers):
    dma = pltpu.SemaphoreType.DMA
    vmem = pl.BlockSpec(memory_space=pltpu.VMEM)
    anywhere = pl.BlockSpec(memory_space=pl.ANY)
    return pl.pallas_call(
        move_kernel,
        out_shape=[jax.ShapeDtypeStruct((2, SPANS, PIECE, HEAD), BF16), jax.ShapeDtypeStruct((SPANS, 2, KEYS, HEAD), BF16),
                   jax.ShapeDtypeStruct((SPANS, ROWS, 2 * HEAD), F32)],
        in_specs=[vmem, anywhere],
        out_specs=[vmem] * 3,
        scratch_shapes=[pltpu.VMEM((TILE, HEAD), BF16), pltpu.SMEM((SPANS + 3, SPANS), jnp.int32),
                        dma((2,)), dma(()), dma(()), dma((3,)), dma((2,)), dma(()), dma((16, 2)), dma(()), dma((16,))],
        compiler_params=pltpu.CompilerParams(collective_id=0, has_side_effects=True, vmem_limit_bytes=24 << 20),
    )(rows, numbers)


def column_to_row(column):
    eye = lax.broadcasted_iota(jnp.int32, column.shape, 0) == lax.broadcasted_iota(jnp.int32, column.shape, 1)
    return jnp.sum(jnp.where(eye, column, 0.0), axis=0, keepdims=True)


def encode(row):
    first = row.astype(BF16).astype(F32)
    second = (row - first).astype(BF16).astype(F32)
    third = (row - first - second).astype(BF16).astype(F32)
    place = lax.broadcasted_iota(jnp.int32, (16, HEAD), 0)
    tile = jnp.where(place == 0, first, jnp.where(place == 1, second, jnp.where(place == 2, third, 0.0)))
    return tile.astype(BF16)


def attend_kernel(table_in, qg, kv, begun, acc, top, table, cells, keep, sem):
    load = pltpu.make_async_copy(table_in, table, sem)
    load.start()
    acc[:SPANS] = begun[...]
    acc[SPANS] = jnp.zeros((ROWS, 2 * HEAD), F32)
    ones = jnp.ones((KEYS, HEAD), BF16)
    qa = lax.axis_index("qa")
    for d in range(SPANS):
        keep[d] = jnp.int32(EARLY)
    begin = jnp.int32(0)
    for i, j in NEAR:
        d = (qa // 4 + i) % 4 * 4 + (qa + j) % 4
        keep[d] = begin
        begin = begin + SPANS - d
    load.wait()

    def gather(skip):
        total = jnp.int32(0)
        for c in range(SPANS):
            for d in range(c + 1):
                cells[total] = c * SPANS + d
                allowed = table[c, d]
                total = total + (jnp.where(keep[d] + (c - d) >= EARLY, allowed, 0) if skip else allowed)
        for n in range(UNROLL - 1):
            cells[total + n] = SPANS * SPANS
        return total

    def operands(n):
        code = cells[n]
        c = code // SPANS
        d = code % SPANS
        cc = jnp.minimum(c, SPANS - 1)
        q = jnp.concatenate([qg[0, cc], qg[1, cc]], axis=0)
        s = lax.dot_general(q, kv[d, 0], (((1,), (1,)), ((), ())), preferred_element_type=F32)
        return c, s, jnp.concatenate([kv[d, 1], ones], axis=1)

    top[...] = jnp.zeros_like(top)
    total = gather(True)

    @pl.loop(0, (total + UNROLL - 1) // UNROLL)
    def _(step):
        group = [operands(step * UNROLL + u) for u in range(UNROLL)]
        sums = [jnp.dot(jnp.exp2(s * SCALE2).astype(BF16), v, preferred_element_type=F32) for c, s, v in group]
        for (c, s, v), term in zip(group, sums):
            acc[c] += term

    sums = acc[:SPANS, :, HEAD:]
    good = jnp.where(jnp.logical_and(sums >= LOWEST, sums <= HIGHEST), 1.0, 0.0)

    @pl.when(jnp.min(good) < 0.5)
    def _():
        top[...] = jnp.full_like(top, -1e30)
        acc[...] = jnp.zeros_like(acc)
        total = gather(False)

        @pl.loop(0, total)
        def _(n):
            c, s, v = operands(n)
            s = s * SCALE
            old = top[c]
            new = jnp.maximum(old, jnp.max(s, axis=1, keepdims=True))
            p = jnp.exp(s - new[:, 0:1]).astype(BF16)
            shrink = jnp.exp(old - new)
            acc[c] = acc[c] * jnp.concatenate([shrink, shrink], axis=1) + jnp.dot(p, v, preferred_element_type=F32)
            top[c] = new


def attend(table, qg, kv, begun):
    vmem = pl.BlockSpec(memory_space=pltpu.VMEM)
    return pl.pallas_call(
        attend_kernel,
        out_shape=[jax.ShapeDtypeStruct((SPANS + 1, ROWS, 2 * HEAD), F32), jax.ShapeDtypeStruct((SPANS + 1, ROWS, HEAD), F32)],
        in_specs=[pl.BlockSpec(memory_space=pl.ANY), vmem, vmem, vmem],
        out_specs=[vmem, vmem],
        scratch_shapes=[pltpu.SMEM((SPANS + 3, SPANS), jnp.int32), pltpu.SMEM((160,), jnp.int32), pltpu.SMEM((SPANS,), jnp.int32), pltpu.SemaphoreType.DMA(())],
        compiler_params=pltpu.CompilerParams(vmem_limit_bytes=24 << 20),
    )(table, qg, kv, begun)


def read_rows(block):
    parts = block.astype(F32)
    return parts[0:1] + parts[1:2] + parts[2:3]


def row_to_column(row):
    eye = lax.broadcasted_iota(jnp.int32, (PIECE, HEAD), 0) == lax.broadcasted_iota(jnp.int32, (PIECE, HEAD), 1)
    return jnp.sum(jnp.where(eye, jnp.broadcast_to(row, (PIECE, HEAD)), 0.0), axis=1, keepdims=True)


def merge_kernel(acc, top, out, part, arrived, m_send, m_recv):
    qa, kb, z, core = coords()
    home = qa // 8
    slot = qa % 8
    mine = z // 2

    barrier = pltpu.get_barrier_semaphore()

    own = jnp.logical_and(home == core, mine == core)
    for t in range(8):
        for n in range(4):
            device = (8 * core + (qa + t) % 8, (z + n) % 4 * 2 + mine)
            if t or n:
                pl.semaphore_signal(barrier, inc=1, device_id=device, device_id_type=MESH)
            else:
                @pl.when(jnp.logical_not(own))
                def _():
                    pl.semaphore_signal(barrier, inc=1, device_id=device, device_id_type=MESH)

    def finish(t):
        c = (qa + t) % SPANS
        for half in range(2):
            rows = pl.ds(half * PIECE, PIECE)
            sums = acc[c, rows, HEAD:]
            part[half, c, 0:PIECE] = (acc[c, rows, :HEAD] / sums).astype(BF16)
            part[half, c, PIECE:] = encode(column_to_row(jnp.log(sums) + top[c, rows]))

    def give(t, n):
        c = (qa + t) % SPANS
        half = (z + n) % 2
        return half, c, remote(part.at[half, c], arrived.at[slot, z], m_send, m_recv, (c, (2 * core + half) * 2 + home))

    def send(t):
        for n in range(2):
            half, c, copy = give(t, n)
            if t or n:
                copy.start()
            else:
                @pl.when(own)
                def _():
                    pltpu.make_async_copy(part.at[half, c], arrived.at[slot, z], m_recv).start()

                @pl.when(jnp.logical_not(own))
                def _():
                    copy.start()

    for t in range(8):
        finish(t)
    pl.semaphore_wait(barrier, 32 - jnp.where(own, 1, 0))
    for t in range(8):
        send(t)
    for block in range(2):
        for t in range(8 + 4 * block, 12 + 4 * block):
            finish(t)
        for t in range(8 + 4 * block, 12 + 4 * block):
            send(t)

    remote(arrived, arrived, m_send, m_recv, (qa, kb)).wait_recv()
    for i in range(8):
        levels = [read_rows(arrived[i, zz, PIECE:]) for zz in range(4)]
        peak = jnp.maximum(jnp.maximum(levels[0], levels[1]), jnp.maximum(levels[2], levels[3]))
        weights = [jnp.exp(level - peak) for level in levels]
        total = weights[0] + weights[1] + weights[2] + weights[3]
        value = None
        for zz in range(4):
            term = row_to_column(weights[zz] / total) * arrived[i, zz, 0:PIECE].astype(F32)
            value = term if value is None else value + term
        out[STARTS[i]:STARTS[i] + PIECE] = value.astype(BF16)

    every = part.at[:]

    @pl.when(own)
    def _():
        remote(part.at[0, pl.ds(1, 15)], part.at[0, pl.ds(1, 15)], m_send, m_recv, (qa, kb)).wait_send()
        remote(part.at[1], part.at[1], m_send, m_recv, (qa, kb)).wait_send()

    @pl.when(jnp.logical_not(own))
    def _():
        remote(every, every, m_send, m_recv, (qa, kb)).wait_send()


def merge(acc, top):
    dma = pltpu.SemaphoreType.DMA
    vmem = pl.BlockSpec(memory_space=pltpu.VMEM)
    block = (PIECE + 16, HEAD)
    return pl.pallas_call(
        merge_kernel,
        out_shape=jax.ShapeDtypeStruct((TILE, HEAD), BF16),
        in_specs=[vmem, vmem],
        out_specs=vmem,
        scratch_shapes=[pltpu.VMEM((2, SPANS) + block, BF16), pltpu.VMEM((8, 4) + block, BF16),
                        dma(()), dma(())],
        compiler_params=pltpu.CompilerParams(collective_id=1, has_side_effects=True, vmem_limit_bytes=24 << 20),
    )(acc, top)


def local(q, k, v, table, fo, ho, wo):
    rows = jnp.stack([q, k, v])
    numbers = jnp.concatenate([table, fo[None], ho[None], wo[None]])
    qg, kv, begun = move(rows, numbers)
    return merge(*attend(numbers, qg, kv, begun))


def solution(mesh):
    rows = P(("qa", "kb"), None)
    return jax.shard_map(local, mesh=mesh, in_specs=(rows, rows, rows, P(), P(), P(), P()), out_specs=rows, check_vma=False)
```

```python
import jax
import jax.numpy as jnp
import numpy as np
from jax import lax
from jax.experimental import pallas as pl
from jax.experimental.pallas import tpu as pltpu
from jax.sharding import PartitionSpec as P

HEIGHT = 32
WIDTH = 52
SPANS = 16
TILE = 624
HEAD = 128
PIECE = 80
STARTS = tuple(16 * (i * 34 // 7) for i in range(8))
MESH = pl.DeviceIdType.MESH
BF16 = jnp.bfloat16
F32 = jnp.float32
ROWS = 2 * PIECE
KEYS = 2 * TILE
UNROLL = 4
SCALE = float(HEAD ** -0.5)
SCALE2 = float(HEAD ** -0.5 * np.log2(np.e))
LOWEST = 1e-25
HIGHEST = 1e30


def coords():
    qa = lax.axis_index("qa")
    kb = lax.axis_index("kb")
    return qa, kb, kb // 2, kb % 2


def turn_table(numbers, qa, kb):
    row = lax.broadcasted_iota(jnp.int32, (TILE, HEAD), 0)
    lane = lax.broadcasted_iota(jnp.int32, (TILE, HEAD), 1) % 64
    within = (row + kb * TILE).astype(F32)
    frame = jnp.floor((within + 0.5) * (1.0 / (HEIGHT * WIDTH)))
    line = jnp.floor((within + 0.5) * (1.0 / WIDTH))
    column = within - line * WIDTH + numbers[SPANS + 2, qa].astype(F32)
    line = line - frame * HEIGHT + numbers[SPANS + 1, qa].astype(F32)
    frame = frame + numbers[SPANS, qa].astype(F32)
    angles = jnp.where(lane < 22, frame, jnp.where(lane < 43, line, column)) * frequencies()
    turns = jnp.floor(angles * np.float32(2 / np.pi) + 0.5)
    rest = angles - turns * np.float32(1.5703125)
    rest = rest - turns * np.float32(4.837512969970703125e-4)
    rest = rest - turns * np.float32(7.54978995489188216e-8)
    sq = rest * rest
    sine = rest + rest * sq * (np.float32(-1 / 6) + sq * (np.float32(8.3333333e-3) + sq * (np.float32(-1.98412698e-4) + sq * np.float32(2.7525562e-6))))
    cosine = 1.0 + sq * (np.float32(-0.5) + sq * (np.float32(4.16666667e-2) + sq * (np.float32(-1.38888889e-3) + sq * (np.float32(2.48015873e-5) + sq * np.float32(-2.7557319e-7)))))
    half = jnp.floor(turns * 0.5)
    odd = (turns - 2.0 * half) > 0.5
    flip = (half - 2.0 * jnp.floor(half * 0.5)) > 0.5
    sign = jnp.where(flip, -1.0, 1.0)
    cos_out = jnp.where(odd, -sine, cosine) * sign
    sin_out = jnp.where(odd, cosine, sine) * sign
    full_lane = lax.broadcasted_iota(jnp.int32, (TILE, HEAD), 1)
    return cos_out, jnp.where(full_lane < 64, -sin_out, sin_out)


def turn(rows, cos_out, sin_out):
    x = rows.astype(F32)
    return (x * cos_out + pltpu.roll(x, 64, 1) * sin_out).astype(BF16)


NEAR = ((0, 0), (3, 0), (0, 3), (1, 0), (0, 1), (2, 0), (0, 2))
EARLY = 28
SLOTS = (0, 1, 1, 1, 1, 1, 1, 1)


def near_order(core):
    return [(jnp.where(core == 0, j, i), jnp.where(core == 0, i, j)) for i, j in NEAR]


def remote(src, dst, send, recv, device):
    return pltpu.make_async_remote_copy(src_ref=src, dst_ref=dst, send_sem=send, recv_sem=recv, device_id=device, device_id_type=MESH)


def move_kernel(rows_in, numbers_in, qg, kv, acc,
                qs, numbers, in_sem, q_send, q_recv, z_send, z_recv, kv_send, kv_recv, t_send, t_recv):
    qa, kb, z, core = coords()
    step_a = 1 + 3 * core
    step_b = 4 - 3 * core
    a = (qa // step_a) % 4
    b = (qa // step_b) % 4
    entry = z // 2 == core
    twin = (qa, z * 2 + 1 - core)
    mine = pl.ds(core * TILE, TILE)

    def at(aa, bb):
        return (aa % 4) * step_a + (bb % 4) * step_b

    barrier = pltpu.get_barrier_semaphore()
    loads = [pltpu.make_async_copy(numbers_in, numbers, in_sem.at[0]),
             pltpu.make_async_copy(rows_in.at[2], kv.at[qa, 1, mine], in_sem.at[1])]
    for load in loads:
        load.start()
    for device in ((at(a + 1, b), kb), (at(a + 3, b), kb), (at(a, b + 1), kb), (at(a, b + 3), kb), twin):
        pl.semaphore_signal(barrier, inc=1, device_id=device, device_id_type=MESH)

    q_home = z * 2 + qa // 8

    @pl.when(entry)
    def _():
        for c in range(SPANS):
            @pl.when(jnp.logical_or(c != qa, q_home != kb))
            def _():
                pl.semaphore_signal(barrier, inc=1, device_id=(c, q_home), device_id_type=MESH)
    for half in range(2):
        @pl.when(2 * core + half != z)
        def _():
            pl.semaphore_signal(barrier, inc=1, device_id=(qa, (2 * core + half) * 2 + core), device_id_type=MESH)
    acc[...] = jnp.zeros_like(acc)
    for load in loads:
        load.wait()
    cos_out, sin_out = turn_table(numbers, qa, kb)
    qs[...] = turn(rows_in[0], cos_out, sin_out)
    kv[qa, 0, mine] = turn(rows_in[1], cos_out, sin_out)
    greeted = 13 + jnp.where(entry, 3, 0) - jnp.where(jnp.logical_and(entry, qa // 8 == core), 1, 0)
    pl.semaphore_wait(barrier, greeted)

    def q_copy(t):
        i = (qa + t) % 8
        rows = pl.ds(pl.multiple_of(16 * (i * 34 // 7), 16), PIECE)
        return rows, remote(qs.at[rows], qg.at[z % 2, qa], q_send, q_recv, (8 * core + i, z * 2 + z // 2))

    to_me = jnp.logical_and(qa // 8 == core, entry)
    for t in range(1, 8):
        q_copy(t)[1].start()

    @pl.when(jnp.logical_not(to_me))
    def _():
        q_copy(0)[1].start()

    @pl.when(to_me)
    def _():
        pltpu.make_async_copy(qs.at[q_copy(0)[0]], qg.at[z % 2, qa], q_recv).start()


    def part_ref(span, part):
        return kv.at[span, part, mine]

    def kv_copy(span, part, device):
        copy = remote(part_ref(span, part), part_ref(span, part), kv_send, kv_recv.at[span, part], device)
        copy.start()

    def kv_wait(span, part):
        remote(part_ref(span, part), part_ref(span, part), kv_send, kv_recv.at[span, part], twin).wait_recv()

    def slot_of(span):
        return span

    def twin_copy(span):
        ref = kv.at[span, :, mine]
        return remote(ref, ref, t_send, t_recv.at[slot_of(span)], twin)

    def twin_wait(span):
        ref = kv.at[span, :, pl.ds((1 - core) * TILE, TILE)]
        remote(ref, ref, t_send, t_recv.at[slot_of(span)], twin).wait_recv()

    up_a, down_a = (at(a + 1, b), kb), (at(a - 1, b), kb)
    up_b, down_b = (at(a, b + 1), kb), (at(a, b - 1), kb)
    for part in (1, 0):
        for device in (up_a, down_a, up_b, down_b):
            kv_copy(qa, part, device)
    twin_copy(qa).start()

    def z_copy(d):
        return remote(qg.at[z % 2], qg.at[z % 2], z_send.at[d - 1], z_recv.at[z % 2], (qa, (kb + 2 * d) % 8))

    @pl.when(entry)
    def _():
        remote(qg.at[z % 2], qg.at[z % 2], q_send, q_recv, twin).wait_recv()
        for d in (2, 1, 3):
            z_copy(d).start()

    def arrive(span, part, devices):
        kv_wait(span, part)
        for device in devices:
            kv_copy(span, part, device)
        if part == 0:
            twin_copy(span).start()

    arrive(at(a - 1, b), 1, (up_a, up_b, down_b))
    arrive(at(a + 1, b), 1, (up_b, down_b))
    arrive(at(a, b - 1), 1, (up_b,))
    arrive(at(a, b + 1), 1, ())
    arrive(at(a - 1, b), 0, (up_b, down_b))
    arrive(at(a + 1, b), 0, (down_a, up_b, down_b))
    arrive(at(a, b - 1), 0, ())
    arrive(at(a, b + 1), 0, (down_b,))
    arrive(at(a + 2, b), 1, (up_b, down_b))
    arrive(at(a + 2, b), 0, (up_b, down_b))
    ones = jnp.ones((KEYS, HEAD), BF16)

    spans = [at(a + i, b + j) for i, j in near_order(core)]
    begins = [jnp.int32(0)]
    for span in spans:
        begins.append(begins[-1] + SPANS - span)

    def cells(n):
        for u in range(UNROLL):
            t = n + u
            d = spans[0]
            c = d + t
            for span, begin in zip(spans[1:], begins[1:]):
                here = t >= begin
                d = jnp.where(here, span, d)
                c = jnp.where(here, span + t - begin, c)
            cc = jnp.minimum(c, SPANS - 1)
            weight = jnp.where(t < begins[-1], numbers[cc, d], 0).astype(F32)
            q = jnp.concatenate([qg[0, cc], qg[1, cc]], axis=0)
            scores = lax.dot_general(q, kv[d, 0], (((1,), (1,)), ((), ())), preferred_element_type=F32)
            p = jnp.exp2(scores * SCALE2).astype(BF16)
            v = jnp.concatenate([kv[d, 1], ones], axis=1)
            acc[cc] += weight * jnp.dot(p, v, preferred_element_type=F32)

    arrive(at(a, b + 2), 1, ())
    arrive(at(a, b + 2), 0, ())
    done = [0]

    def next_cells(n):
        start = done[0]
        done[0] = min(EARLY // UNROLL, start + n)

        @pl.loop(start, done[0])
        def _(step):
            cells(step * UNROLL)

    def events(step, middle, last):
        arrive(at(a + step, b - 1), 1, (up_b,))
        arrive(at(a + step, b + 1), 1, ())
        next_cells(middle)
        arrive(at(a + step, b - 1), 0, ())
        arrive(at(a + step, b + 1), 0, (down_b,))
        next_cells(last)

    events(3, 0, 0)
    for half in range(2):
        @pl.when(jnp.logical_or(jnp.logical_not(entry), half != z % 2))
        def _():
            remote(qg.at[half], qg.at[half], z_send.at[0], z_recv.at[half], twin).wait_recv()
    for i, j in NEAR:
        twin_wait(at(a + i, b + j))
    next_cells(SLOTS[0])
    events(1, SLOTS[1], SLOTS[2])
    events(2, SLOTS[3], SLOTS[4])
    for step, slot in ((3, 5), (1, 6), (2, 7)):
        next_cells(SLOTS[slot])
        arrive(at(a + step, b + 2), 1, ())
        arrive(at(a + step, b + 2), 0, ())
    for i in (0, 3, 1, 2):
        for j in (0, 3, 1, 2):
            if (i, j) not in NEAR:
                twin_wait(at(a + i, b + j))

    @pl.when(entry)
    def _():
        for d in (1, 2, 3):
            z_copy(d).wait_send()
    @pl.when(to_me)
    def _():
        remote(qg.at[0, pl.ds(0, 7)], qg.at[0, pl.ds(0, 7)], q_send, q_recv, twin).wait_send()

    @pl.when(jnp.logical_not(to_me))
    def _():
        remote(qg.at[0, pl.ds(0, 8)], qg.at[0, pl.ds(0, 8)], q_send, q_recv, twin).wait_send()
    ref = kv.at[pl.ds(0, 15), :, mine]
    remote(ref, ref, kv_send, kv_recv.at[0, 0], twin).wait_send()
    ref = kv.at[:, :, mine]
    remote(ref, ref, t_send, t_recv.at[0], twin).wait_send()


def frequencies():
    lead = 1.0 / 10000.0 ** (np.arange(22, dtype=np.float32) / np.float32(22))
    side = 1.0 / 10000.0 ** (np.arange(21, dtype=np.float32) / np.float32(21))
    lane = lax.broadcasted_iota(jnp.int32, (1, HEAD), 1) % 64
    row = jnp.zeros((1, HEAD), F32)
    for n, value in enumerate(np.concatenate([lead, side, side])):
        row = jnp.where(lane == n, np.float32(value), row)
    return row


def move(rows, numbers):
    dma = pltpu.SemaphoreType.DMA
    vmem = pl.BlockSpec(memory_space=pltpu.VMEM)
    anywhere = pl.BlockSpec(memory_space=pl.ANY)
    return pl.pallas_call(
        move_kernel,
        out_shape=[jax.ShapeDtypeStruct((2, SPANS, PIECE, HEAD), BF16), jax.ShapeDtypeStruct((SPANS, 2, KEYS, HEAD), BF16),
                   jax.ShapeDtypeStruct((SPANS + 1, ROWS, 2 * HEAD), F32)],
        in_specs=[vmem, anywhere],
        out_specs=[vmem] * 3,
        scratch_shapes=[pltpu.VMEM((TILE, HEAD), BF16), pltpu.SMEM((SPANS + 3, SPANS), jnp.int32),
                        dma((2,)), dma(()), dma(()), dma((3,)), dma((2,)), dma(()), dma((16, 2)), dma(()), dma((16,))],
        compiler_params=pltpu.CompilerParams(collective_id=0, has_side_effects=True, vmem_limit_bytes=24 << 20),
    )(rows, numbers)


def column_to_row(column):
    eye = lax.broadcasted_iota(jnp.int32, column.shape, 0) == lax.broadcasted_iota(jnp.int32, column.shape, 1)
    return jnp.sum(jnp.where(eye, column, 0.0), axis=0, keepdims=True)


def encode(row):
    first = row.astype(BF16).astype(F32)
    second = (row - first).astype(BF16).astype(F32)
    third = (row - first - second).astype(BF16).astype(F32)
    place = lax.broadcasted_iota(jnp.int32, (16, HEAD), 0)
    tile = jnp.where(place == 0, first, jnp.where(place == 1, second, jnp.where(place == 2, third, 0.0)))
    return tile.astype(BF16)


def attend_kernel(table_in, qg, kv, begun, acc, top, table, cells, keep, sem):
    load = pltpu.make_async_copy(table_in, table, sem)
    load.start()
    ones = jnp.ones((KEYS, HEAD), BF16)
    qa = lax.axis_index("qa")
    for d in range(SPANS):
        keep[d] = jnp.int32(EARLY)
    begin = jnp.int32(0)
    for i, j in NEAR:
        d = (qa // 4 + i) % 4 * 4 + (qa + j) % 4
        keep[d] = begin
        begin = begin + SPANS - d
    load.wait()

    def gather(skip):
        total = jnp.int32(0)
        for c in range(SPANS):
            for d in range(c + 1):
                cells[total] = c * SPANS + d
                allowed = table[c, d]
                total = total + (jnp.where(keep[d] + (c - d) >= EARLY, allowed, 0) if skip else allowed)
        for n in range(UNROLL - 1):
            cells[total + n] = SPANS * SPANS
        return total

    def operands(n):
        code = cells[n]
        c = code // SPANS
        d = code % SPANS
        cc = jnp.minimum(c, SPANS - 1)
        q = jnp.concatenate([qg[0, cc], qg[1, cc]], axis=0)
        s = lax.dot_general(q, kv[d, 0], (((1,), (1,)), ((), ())), preferred_element_type=F32)
        return c, s, jnp.concatenate([kv[d, 1], ones], axis=1)

    top[...] = jnp.zeros_like(top)
    total = gather(True)

    @pl.loop(0, (total + UNROLL - 1) // UNROLL)
    def _(step):
        group = [operands(step * UNROLL + u) for u in range(UNROLL)]
        sums = [jnp.dot(jnp.exp2(s * SCALE2).astype(BF16), v, preferred_element_type=F32) for c, s, v in group]
        for (c, s, v), term in zip(group, sums):
            acc[c] += term

    sums = acc[:SPANS, :, HEAD:]
    good = jnp.where(jnp.logical_and(sums >= LOWEST, sums <= HIGHEST), 1.0, 0.0)

    @pl.when(jnp.min(good) < 0.5)
    def _():
        top[...] = jnp.full_like(top, -1e30)
        acc[...] = jnp.zeros_like(acc)
        total = gather(False)

        @pl.loop(0, total)
        def _(n):
            c, s, v = operands(n)
            s = s * SCALE
            old = top[c]
            new = jnp.maximum(old, jnp.max(s, axis=1, keepdims=True))
            p = jnp.exp(s - new[:, 0:1]).astype(BF16)
            shrink = jnp.exp(old - new)
            acc[c] = acc[c] * jnp.concatenate([shrink, shrink], axis=1) + jnp.dot(p, v, preferred_element_type=F32)
            top[c] = new


def attend(table, qg, kv, begun):
    vmem = pl.BlockSpec(memory_space=pltpu.VMEM)
    return pl.pallas_call(
        attend_kernel,
        out_shape=[jax.ShapeDtypeStruct((SPANS + 1, ROWS, 2 * HEAD), F32), jax.ShapeDtypeStruct((SPANS + 1, ROWS, HEAD), F32)],
        in_specs=[pl.BlockSpec(memory_space=pl.ANY), vmem, vmem, vmem],
        out_specs=[vmem, vmem],
        input_output_aliases={3: 0},
        scratch_shapes=[pltpu.SMEM((SPANS + 3, SPANS), jnp.int32), pltpu.SMEM((160,), jnp.int32), pltpu.SMEM((SPANS,), jnp.int32), pltpu.SemaphoreType.DMA(())],
        compiler_params=pltpu.CompilerParams(vmem_limit_bytes=24 << 20),
    )(table, qg, kv, begun)


def read_rows(block):
    parts = block.astype(F32)
    return parts[0:1] + parts[1:2] + parts[2:3]


def row_to_column(row):
    eye = lax.broadcasted_iota(jnp.int32, (PIECE, HEAD), 0) == lax.broadcasted_iota(jnp.int32, (PIECE, HEAD), 1)
    return jnp.sum(jnp.where(eye, jnp.broadcast_to(row, (PIECE, HEAD)), 0.0), axis=1, keepdims=True)


def merge_kernel(acc, top, out, part, arrived, m_send, m_recv):
    qa, kb, z, core = coords()
    home = qa // 8
    slot = qa % 8
    mine = z // 2

    barrier = pltpu.get_barrier_semaphore()

    own = jnp.logical_and(home == core, mine == core)
    for t in range(8):
        for n in range(4):
            device = (8 * core + (qa + t) % 8, (z + n) % 4 * 2 + mine)
            if t or n:
                pl.semaphore_signal(barrier, inc=1, device_id=device, device_id_type=MESH)
            else:
                @pl.when(jnp.logical_not(own))
                def _():
                    pl.semaphore_signal(barrier, inc=1, device_id=device, device_id_type=MESH)

    def finish(t):
        c = (qa + t) % SPANS
        for half in range(2):
            rows = pl.ds(half * PIECE, PIECE)
            sums = acc[c, rows, HEAD:]
            part[half, c, 0:PIECE] = (acc[c, rows, :HEAD] / sums).astype(BF16)
            part[half, c, PIECE:] = encode(column_to_row(jnp.log(sums) + top[c, rows]))

    def give(t, n):
        c = (qa + t) % SPANS
        half = (z + n) % 2
        return half, c, remote(part.at[half, c], arrived.at[slot, z], m_send, m_recv, (c, (2 * core + half) * 2 + home))

    def send(t):
        for n in range(2):
            half, c, copy = give(t, n)
            if t or n:
                copy.start()
            else:
                @pl.when(own)
                def _():
                    pltpu.make_async_copy(part.at[half, c], arrived.at[slot, z], m_recv).start()

                @pl.when(jnp.logical_not(own))
                def _():
                    copy.start()

    for t in range(8):
        finish(t)
    pl.semaphore_wait(barrier, 32 - jnp.where(own, 1, 0))
    for t in range(8):
        send(t)
    for block in range(2):
        for t in range(8 + 4 * block, 12 + 4 * block):
            finish(t)
        for t in range(8 + 4 * block, 12 + 4 * block):
            send(t)

    remote(arrived, arrived, m_send, m_recv, (qa, kb)).wait_recv()
    for i in range(8):
        levels = [read_rows(arrived[i, zz, PIECE:]) for zz in range(4)]
        peak = jnp.maximum(jnp.maximum(levels[0], levels[1]), jnp.maximum(levels[2], levels[3]))
        weights = [jnp.exp(level - peak) for level in levels]
        total = weights[0] + weights[1] + weights[2] + weights[3]
        value = None
        for zz in range(4):
            term = row_to_column(weights[zz] / total) * arrived[i, zz, 0:PIECE].astype(F32)
            value = term if value is None else value + term
        out[STARTS[i]:STARTS[i] + PIECE] = value.astype(BF16)

    every = part.at[:]

    @pl.when(own)
    def _():
        remote(part.at[0, pl.ds(1, 15)], part.at[0, pl.ds(1, 15)], m_send, m_recv, (qa, kb)).wait_send()
        remote(part.at[1], part.at[1], m_send, m_recv, (qa, kb)).wait_send()

    @pl.when(jnp.logical_not(own))
    def _():
        remote(every, every, m_send, m_recv, (qa, kb)).wait_send()


def merge(acc, top):
    dma = pltpu.SemaphoreType.DMA
    vmem = pl.BlockSpec(memory_space=pltpu.VMEM)
    block = (PIECE + 16, HEAD)
    return pl.pallas_call(
        merge_kernel,
        out_shape=jax.ShapeDtypeStruct((TILE, HEAD), BF16),
        in_specs=[vmem, vmem],
        out_specs=vmem,
        scratch_shapes=[pltpu.VMEM((2, SPANS) + block, BF16), pltpu.VMEM((8, 4) + block, BF16),
                        dma(()), dma(())],
        compiler_params=pltpu.CompilerParams(collective_id=1, has_side_effects=True, vmem_limit_bytes=24 << 20),
    )(acc, top)


def local(q, k, v, table, fo, ho, wo):
    rows = jnp.stack([q, k, v])
    numbers = jnp.concatenate([table, fo[None], ho[None], wo[None]])
    qg, kv, begun = move(rows, numbers)
    return merge(*attend(numbers, qg, kv, begun))


def solution(mesh):
    rows = P(("qa", "kb"), None)
    return jax.shard_map(local, mesh=mesh, in_specs=(rows, rows, rows, P(), P(), P(), P()), out_specs=rows, check_vma=False)
```
